512 devices in a mesh: tm: 16 (over z_lo, x), space: 32 (over z_hi, y, core).
Axes of the slice: x: 4, y: 4, z: 16 (z_hi: 4, z_lo: 4; z = z_hi * 4 + z_lo), core: 2. Of those that a mesh axis runs over, the one named last changes fastest.
Arguments:
- start_state: float32 [16, 3, 16, 512, 128], P('tm', None, None, 'space'), may hold values from -6 to 6
- land_mask: int32 [512, 128], P('space'), may hold values 0 or 1
- fold_map: int32 [128], replicated, may hold values from 0 to 127, as said below
- coupling: float32 [16, 16], replicated, may hold values from -1 to 1, as said below
- depths: float32 [16], replicated, may hold values from 0.2 to 0.5
Outputs:
- next_state: float32 [16, 3, 16, 512, 128], P('tm', None, None, 'space')
The draws below stay inside these ranges and needn't reach their ends.
Inputs may be any that keep to these rules, and one draw needn't show every extreme that they name: fold_map[i] = (q - i) mod 128 for one q with q % 4 == 3. `coupling`: symmetric; every diagonal entry exceeds the sum of the magnitudes of the other entries of its row.
All inputs are finite; a program needn't handle non-finite values. No bound on the sum of `land_mask` on one device may be relied on, other than what follows from the above.
Results may differ from the reference program's by a relative error of at most 0.0002.
Values sent between devices are 32-bit elements; how exact they have to be, the bound alone decides.
No kernel may reach another device: no remote copies, remote signals or barrier semaphores. Data moves between devices by JAX's collectives and lax.ppermute only.
A program may use at most 64 MiB of HBM per device.

```python
import math
import jax
import jax.numpy as jnp
from jax import lax

LAYERS = 16
ZONAL = 128
FINE_STEPS = 8
COARSE_STEPS = 2
SLICES = 16
GRID_ROWS = 512


def draw_fold_map(key, part):
    key = jax.random.fold_in(key, 23)
    centre = jax.random.randint(key, (), 0, ZONAL // 4)
    columns = jnp.arange(ZONAL, dtype=jnp.int32)
    return ((4 * centre + 3 - columns) % ZONAL).astype(jnp.int32)


def draw_coupling(key, part):
    key = jax.random.fold_in(key, 11)
    key_diagonal, key_size, key_sign = jax.random.split(key, 3)
    diagonal = jax.random.uniform(key_diagonal, (LAYERS,), jnp.float32, 0.5, 1.0)
    magnitude = jax.random.uniform(key_size, (LAYERS, LAYERS), jnp.float32, 0.5, 1.0)
    sign_choice = jnp.where(jax.random.bernoulli(key_sign, 0.5, (LAYERS, LAYERS)), 1.0, -1.0)
    upper_part = jnp.triu(magnitude * sign_choice, 1) * (0.45 / max(LAYERS - 1, 1))
    return (jnp.diag(diagonal) + upper_part + upper_part.T).astype(jnp.float32)


def place_ends(values, rng, smallest, largest):
    spot = [jax.random.randint(jax.random.fold_in(rng, axis), (), 0, length) for axis, length in enumerate(values.shape)]
    longest = values.shape.index(max(values.shape))
    beside = spot[:longest] + [(spot[longest] + 1) % values.shape[longest]] + spot[longest + 1:]
    return values.at[tuple(spot)].set(smallest).at[tuple(beside)].set(largest)


def block_scale(stream_key, dims, shards, low, top_value):
    def one(position, shards_of):
        heights = jax.random.uniform(jax.random.fold_in(jax.random.fold_in(stream_key, 6), position), (shards_of,), jnp.float32, low / len(shards), top_value / len(shards))
        return jnp.repeat(jnp.exp(heights), dims[position] // shards_of).reshape((-1,) + (1,) * (len(dims) - position - 1))

    loudness = one(*shards[0])
    for cut in shards[1:]:
        loudness = loudness * one(*cut)
    return loudness


def normal_values(stream_key, shape, width, bound, pieces=(), held_as=jnp.bfloat16):
    loudness = block_scale(stream_key, shape, pieces, -0.22, 0.18) if pieces else 1.0
    drawn = jax.random.normal(stream_key, shape, jnp.float32) * width * loudness
    return jnp.minimum(jnp.maximum(drawn, -bound), bound).astype(held_as)


def setup_inputs(seed: int = 0) -> dict:
    splits = jax.random.split(jax.random.key(seed), 6)
    return {
        "start_state": normal_values(splits[0], (SLICES, 3, LAYERS, GRID_ROWS, ZONAL), 1.0, 6.0, ((0, 16), (3, 32)), jnp.float32),
        "land_mask": place_ends((jax.random.randint(splits[1], (GRID_ROWS, ZONAL), 0, 5) < 4).astype(jnp.int32), jax.random.fold_in(splits[1], 1), 0, 1),
        "fold_map": draw_fold_map(jax.random.fold_in(splits[5], 71), 0),
        "coupling": draw_coupling(jax.random.fold_in(splits[5], 71), 0),
        "depths": jnp.clip(jnp.exp(jax.random.uniform(splits[4], (LAYERS,), jnp.float32, math.log(0.2), math.log(0.5))), 0.2, 0.5),
    }


FRICTION = 0.02


def coriolis_rows(offset, count, extent):
    positions = (jnp.arange(count, dtype=jnp.int32) + offset).astype(jnp.float32)
    latitude = (positions + 0.5) / extent
    latitude = jnp.where(latitude > 1.0, 2.0 - latitude, latitude)
    return 0.3 * (latitude - 0.5)


def advance(extended, mask_rows, coriolis, coupling, depths, step_size):
    thickness, eastward, northward = extended[0], extended[1], extended[2]
    pressure = jnp.einsum("lm,mrc->lrc", coupling, thickness, precision=lax.Precision.HIGHEST)
    gradient_east = jnp.roll(pressure, -1, axis=-1) - jnp.roll(pressure, 1, axis=-1)
    gradient_north = pressure[:, 2:] - pressure[:, :-2]
    wet_rows = mask_rows[1:-1]
    coriolis_mid = coriolis[1:-1, None]
    eastward_old = eastward[:, 1:-1]
    northward_old = northward[:, 1:-1]
    eastward_new = wet_rows * (eastward_old + step_size * (coriolis_mid * northward_old - FRICTION * eastward_old) - 0.5 * gradient_east[:, 1:-1])
    northward_new = wet_rows * (northward_old - step_size * (coriolis_mid * eastward_new + FRICTION * northward_old) - 0.5 * gradient_north)
    spreading = (jnp.roll(eastward_new, -1, axis=-1) - jnp.roll(eastward_new, 1, axis=-1))[:, 1:-1] + northward_new[:, 2:] - northward_new[:, :-2]
    thickness_new = mask_rows[2:-2] * (thickness[:, 2:-2] - 0.5 * depths[:, None, None] * spreading)
    return jnp.stack([thickness_new, eastward_new[:, 1:-1], northward_new[:, 1:-1]])


def pad_rows(values, rim_width, fold_map, parity):
    interior = values[..., values.shape[-2] - rim_width:, :][..., ::-1, :]
    folded = jnp.take(interior, fold_map, axis=-1) * parity
    bottom_rows = jnp.zeros_like(values[..., :rim_width, :])
    return jnp.concatenate([bottom_rows, values, folded], axis=-2)


def restrict(values):
    layout = values.shape
    blocks = values.reshape(layout[:-2] + (layout[-2] // 4, 4, layout[-1] // 4, 4))
    return jnp.mean(blocks, axis=(-3, -1))


def prolong(values):
    return jnp.repeat(jnp.repeat(values, 4, axis=-2), 4, axis=-1)


def reference(start_state, land_mask, fold_map, coupling, depths):
    parity = jnp.array([1.0, -1.0, -1.0], jnp.float32).reshape(3, 1, 1, 1)
    wet = land_mask.astype(jnp.float32)
    grid_rows = wet.shape[0]
    coarse_fold = (fold_map[0::4] // 4).astype(jnp.int32)
    fine_mask = pad_rows(wet, 2, fold_map, 1.0)
    fine_coriolis = coriolis_rows(-2, grid_rows + 4, float(grid_rows))
    coarse_width = 2 * COARSE_STEPS
    coarse_rows = grid_rows // 4
    coarse_mask = pad_rows(restrict(wet), coarse_width, coarse_fold, 1.0)
    coarse_coriolis = coriolis_rows(-coarse_width, coarse_rows + 2 * coarse_width, float(coarse_rows))

    def fine_run(initial):
        current = initial
        for substep in range(FINE_STEPS):
            extended = pad_rows(current, 2, fold_map, parity)
            current = advance(extended, fine_mask, fine_coriolis, coupling, depths, 1.0)
        return current

    def coarse_run(initial):
        extended = pad_rows(initial, coarse_width, coarse_fold, parity)
        length = coarse_mask.shape[0]
        for substep in range(COARSE_STEPS):
            extended = advance(extended, coarse_mask[2 * substep: length - 2 * substep], coarse_coriolis[2 * substep: length - 2 * substep], coupling, depths, 4.0)
        return extended

    fine = lax.map(fine_run, start_state)
    coarse_old = lax.map(lambda initial: coarse_run(restrict(initial)), start_state)
    discrepancy = restrict(fine) - coarse_old

    def chain_turn(current, inputs):
        slice_gap, slice_fine = inputs
        following = coarse_run(current) + slice_gap
        return following, slice_fine + prolong(following - restrict(slice_fine))

    unused, next_state = lax.scan(chain_turn, restrict(start_state[0]), (discrepancy, fine))
    return next_state
```

```python
import functools

import jax
import jax.numpy as jnp
from jax import lax
from jax.experimental import pallas as pl
from jax.experimental.pallas import tpu as pltpu
from jax.sharding import Mesh
from jax.sharding import PartitionSpec as P

LAYERS = 16
ZONAL = 128
FINE_STEPS = 8
BAND = 16
BANDS = 32
EXTENT = BAND * BANDS
HALO = 2 * FINE_STEPS
SPAN = BAND + 2 * HALO
PAD = 4
FRICTION = 0.02
HIGHEST = lax.Precision.HIGHEST
F32 = jnp.float32
BF16 = jnp.bfloat16

SPACE = ("zh", "y", "c")
TIME = ("zl", "x")
PLANE = ("x", "y", "c")

SWEEPS = 6
SHIFT = 1.0


def iota(shape, axis):
    return lax.broadcasted_iota(jnp.int32, shape, axis)


def block_mean_matrix():
    row = iota((4 * ZONAL, ZONAL), 0)
    col = iota((4 * ZONAL, ZONAL), 1)
    target = (row // ZONAL) * 32 + (row % ZONAL) // 4
    return jnp.where(col == target, 1.0 / 16.0, 0.0).astype(F32)


def restrict_kernel(own, out, sums):
    for f in range(3):
        for cr in range(4):
            total = None
            for r in range(4):
                row = own[pl.ds(f * 256 + 4 * cr + r, LAYERS, stride=BAND), :]
                total = row if total is None else total + row
            sums[f * LAYERS : (f + 1) * LAYERS, cr * ZONAL : (cr + 1) * ZONAL] = total
    out[...] = jnp.dot(sums[...], block_mean_matrix(), precision=HIGHEST, preferred_element_type=F32)


def swap_rows(x, k):
    halves = [x[:8], x[8:]]
    if k & 8:
        halves = halves[::-1]
    done = []
    for y in halves:
        sub = iota(y.shape, 0)
        if k & 4:
            y = pltpu.roll(y, 4, 0)
        if k & 2:
            y = jnp.where((sub & 2) == 0, pltpu.roll(y, 6, 0), pltpu.roll(y, 2, 0))
        if k & 1:
            y = jnp.where((sub & 1) == 0, pltpu.roll(y, 7, 0), pltpu.roll(y, 1, 0))
        done.append(y)
    return jnp.concatenate(done, axis=0)


def modes_kernel(coupling, depths, vectors, values):
    row = iota((LAYERS, ZONAL), 0)
    lane = iota((LAYERS, ZONAL), 1)
    eye = row == lane
    root = jnp.sqrt(depths[...])
    root = jnp.concatenate([root, jnp.zeros((1, ZONAL - LAYERS), F32)], axis=1)
    root_lanes = jnp.broadcast_to(root, (LAYERS, ZONAL))
    root_rows = jnp.sum(jnp.where(eye, root_lanes, 0.0), axis=1, keepdims=True)
    matrix = jnp.concatenate([coupling[...], jnp.zeros((LAYERS, ZONAL - LAYERS), F32)], axis=1)
    matrix = matrix * root_lanes * root_rows
    start = matrix + jnp.where(eye, SHIFT, 0.0) + jnp.where(lane == row + LAYERS, 1.0, 0.0)
    active = lane < LAYERS

    def sweep(_, x):
        size = jnp.sum(jnp.where(active, x * x, 0.0), axis=1, keepdims=True)
        size = jnp.broadcast_to(size, x.shape)
        for k in range(1, LAYERS):
            other = swap_rows(x, k)
            other_size = swap_rows(size, k)
            inner = jnp.sum(jnp.where(active, x * other, 0.0), axis=1, keepdims=True)
            inner = jnp.broadcast_to(inner, x.shape)
            gap = other_size - size
            first = (row & (1 << (k.bit_length() - 1))) == 0
            sign = jnp.where(gap > 0.0, 1.0, jnp.where(gap < 0.0, -1.0, jnp.where(first, 1.0, -1.0)))
            below = jnp.abs(gap) + jnp.sqrt(gap * gap + 4.0 * inner * inner)
            tangent = jnp.where(below > 0.0, 2.0 * inner * sign / jnp.maximum(below, 1e-30), 0.0)
            cosine = lax.rsqrt(1.0 + tangent * tangent)
            x = cosine * (x - tangent * other)
            size = size - tangent * inner
        return x

    x = lax.fori_loop(0, SWEEPS, sweep, start)
    turned = pltpu.roll(x, ZONAL - LAYERS, 1)
    vectors[...] = jnp.where(active, turned, 0.0)
    value = jnp.sum(jnp.where(active, x * turned, 0.0), axis=1, keepdims=True) - SHIFT
    values[...] = jnp.broadcast_to(value, (LAYERS, ZONAL))


def fine_kernel(
    place, own, low, high, mask_own, mask_low, mask_high, fold, coupling, depths, vectors, following,
    fine, chunk, hs, us, vs, ps, ms, fs, sums,
):
    position = place[0]
    on_top = position == BANDS - 1
    fields = (hs, us, vs)

    def put(field, row, value):
        fields[field][row] = value.reshape(2, 8, ZONAL)

    def mask_put(row, value):
        ms[row] = jnp.broadcast_to(value, (8, ZONAL))

    for f in range(3):
        for r in range(BAND):
            here = pl.ds(f * 256 + r, LAYERS, stride=BAND)
            put(f, PAD + r, low[here, :])
            put(f, PAD + HALO + r, own[here, :])
    for r in range(BAND):
        mask_put(PAD + r, mask_low[r : r + 1, :].astype(F32))
        mask_put(PAD + HALO + r, mask_own[r : r + 1, :].astype(F32))

    @pl.when(jnp.logical_not(on_top))
    def _():
        for f in range(3):
            for r in range(BAND):
                put(f, PAD + HALO + BAND + r, high[pl.ds(f * 256 + r, LAYERS, stride=BAND), :])
        for r in range(BAND):
            mask_put(PAD + HALO + BAND + r, mask_high[r : r + 1, :].astype(F32))

    @pl.when(on_top)
    def _():
        index = jnp.broadcast_to(fold[...], (LAYERS, ZONAL))
        for f in range(3):
            for r in range(BAND):
                facing = own[pl.ds(f * 256 + BAND - 1 - r, LAYERS, stride=BAND), :]
                facing = jnp.take_along_axis(facing, index, axis=1)
                put(f, PAD + HALO + BAND + r, facing if f == 0 else -facing)
        for r in range(BAND):
            facing = jnp.broadcast_to(mask_own[BAND - 1 - r : BAND - r, :].astype(F32), (8, ZONAL))
            ms[PAD + HALO + BAND + r] = jnp.take_along_axis(facing, index[:8], axis=1)

    rows = iota((SPAN + 2 * PAD, 8, ZONAL), 0) + (position * BAND - HALO - PAD)
    latitude = (rows.astype(F32) + 0.5) / float(EXTENT)
    latitude = jnp.where(latitude > 1.0, 2.0 - latitude, latitude)
    fs[...] = 0.3 * (latitude - 0.5)

    half = 0.5 * coupling[...]
    half_top = half.astype(BF16)
    half_rest = (half - half_top.astype(F32)).astype(BF16)
    weights = jnp.concatenate([half_top, half_top, half_rest], axis=1)
    lanes = jnp.broadcast_to(depths[...], (LAYERS, LAYERS))
    eye = iota((LAYERS, LAYERS), 0) == iota((LAYERS, LAYERS), 1)
    thick = 0.5 * jnp.sum(jnp.where(eye, lanes, 0.0), axis=1, keepdims=True)
    thick = jnp.broadcast_to(thick, (LAYERS, ZONAL)).reshape(1, 2, 8, ZONAL)
    keep = 1.0 - FRICTION

    def east(x):
        flat = x.reshape(-1, ZONAL)
        return (pltpu.roll(flat, ZONAL - 1, 1) - pltpu.roll(flat, 1, 1)).reshape(x.shape)

    for step in range(FINE_STEPS):
        first, last = PAD + 2 * step, PAD + SPAN - 2 * step
        for j in range(first, last, 4):
            group = [hs[j + i].reshape(LAYERS, ZONAL) for i in range(4)]
            wide = jnp.concatenate(group, axis=1)
            top = wide.astype(BF16)
            rest = (wide - top.astype(F32)).astype(BF16)
            stacked = jnp.concatenate([top, rest, top], axis=0)
            result = jnp.dot(weights, stacked, preferred_element_type=F32)
            for i in range(4):
                ps[j + i] = result[:, i * ZONAL : (i + 1) * ZONAL].reshape(2, 8, ZONAL)
        for j in range(first + 1, last - 1, 2):
            m = ms[j : j + 2][:, None]
            f = fs[j : j + 2][:, None]
            p = ps[j : j + 2]
            u = us[j : j + 2]
            v = vs[j : j + 2]
            u = m * (keep * u + f * v - east(p))
            v = m * (keep * v - f * u - (ps[j + 1 : j + 3] - ps[j - 1 : j + 1]))
            us[j : j + 2] = u
            vs[j : j + 2] = v
        for j in range(first + 2, last - 2, 2):
            m = ms[j : j + 2][:, None]
            spread = east(us[j : j + 2]) + (vs[j + 1 : j + 3] - vs[j - 1 : j + 1])
            hs[j : j + 2] = m * (hs[j : j + 2] - thick * spread)

    begin = PAD + HALO
    for f in range(3):
        for cr in range(4):
            total = None
            for r in range(4):
                row = fields[f][begin + 4 * cr + r].reshape(LAYERS, ZONAL)
                fine[f * BAND + 4 * cr + r] = row
                total = row if total is None else total + row
            sums[f * LAYERS : (f + 1) * LAYERS, cr * ZONAL : (cr + 1) * ZONAL] = total
    for cr in range(4):
        total = None
        for r in range(4):
            row = ms[begin + 4 * cr + r]
            total = row if total is None else total + row
        sums[3 * LAYERS :, cr * ZONAL : (cr + 1) * ZONAL] = total
    mean = jnp.dot(sums[...], block_mean_matrix(), precision=HIGHEST, preferred_element_type=F32)
    jump = mean[: 3 * LAYERS] - following[...]
    root = jnp.sqrt(depths[...])
    for f in range(3):
        basis = vectors[:, :LAYERS] / root if f == 0 else vectors[:, :LAYERS] * root
        in_modes = jnp.dot(
            basis, jump[f * LAYERS : (f + 1) * LAYERS], precision=HIGHEST, preferred_element_type=F32
        )
        chunk[pl.ds(f, LAYERS, stride=8), :] = in_modes
        chunk[pl.ds(4 + f, LAYERS, stride=8), :] = in_modes
    chunk[pl.ds(3, BANDS, stride=4), :] = jnp.broadcast_to(mean[3 * LAYERS : 3 * LAYERS + 1], (BANDS, ZONAL))


def coarse_tools(value, mask, fold):
    row = iota((32, ZONAL), 0)
    lane = iota((32, ZONAL), 1)
    seg = lane // 32
    col = lane % 32
    after = seg * 32 + (col + 1) % 32
    before = seg * 32 + (col + 31) % 32
    position = (seg * 32 + row).astype(F32)
    coriolis = (4.0 * 0.3) * ((position + 0.5) / float(EXTENT // 4) - 0.5)
    keep = 1.0 - 4.0 * FRICTION
    sub = iota((8, ZONAL), 0)
    seg8 = seg[:8]
    k = fold[0, 0] // 4
    fold_index = 96 + (k - iota((8, ZONAL), 1) + 128) % 32

    def gather(x, index):
        return jnp.take_along_axis(x, index, axis=1)

    def east(x):
        return gather(x, after) - gather(x, before)

    def north(x, sign):
        up = pltpu.roll(x, 31, 0)
        down = pltpu.roll(x, 1, 0)
        mirror = sign * gather(x[24:], fold_index)
        edge = jnp.where(seg8 == 3, mirror, pltpu.roll(up[24:], 96, 1))
        up = jnp.concatenate([up[:24], jnp.where(sub == 7, edge, up[24:])], axis=0)
        edge = jnp.where(seg8 == 0, 0.0, pltpu.roll(down[:8], 32, 1))
        down = jnp.concatenate([jnp.where(sub == 0, edge, down[:8]), down[8:]], axis=0)
        return up - down

    def propagate(h, u, v):
        for _ in range(2):
            p = (0.5 * value) * h
            u = mask * (keep * u + coriolis * v - east(p))
            v = mask * (keep * v - coriolis * u - north(p, 1.0))
            h = mask * (h - 0.5 * (east(u) + north(v, -1.0)))
        return h, u, v

    return propagate


def pair_kernel(place, gathered, values, fold, jumps, mask_out, total):
    lane = iota((8, ZONAL), 1)
    seg = lane // 32
    mode = place[1]
    for x in range(2):
        for f in range(4 if x == 0 else 3):
            rows = [None] * 4
            for zh in range(4):
                piece = gathered[pl.ds(zh * 64 + x * 32 + f, 8, stride=4), :]
                for cr in range(4):
                    shift = (32 * (zh - cr)) % ZONAL
                    moved = pltpu.roll(piece, shift, 1) if shift else piece
                    rows[cr] = moved if zh == 0 else jnp.where(seg == zh, moved, rows[cr])
            for cr in range(4):
                if f == 3:
                    mask_out[pl.ds(cr, 8, stride=4), :] = rows[cr]
                else:
                    jumps[pl.ds((x * 3 + f) * 32 + cr, 8, stride=4), :] = rows[cr]
    propagate = coarse_tools(values[pl.ds(mode, 1), :], mask_out[...], fold)
    state = propagate(*(jumps[f * 32 : (f + 1) * 32, :] for f in range(3)))
    for f in range(3):
        result = state[f] + jumps[(3 + f) * 32 : (4 + f) * 32, :]
        for copy in range(8):
            total[(copy * 3 + f) * 32 : (copy * 3 + f + 1) * 32, :] = result


def chain_kernel(place, totals, jumps, mask, values, fold, chunk, held):
    mode = place[1]
    pair = place[2]
    quarter = place[3]
    core = place[4]
    propagate = coarse_tools(values[pl.ds(mode, 1), :], mask[...], fold)

    def turn(index, state):
        state = propagate(*propagate(*state))
        return tuple(
            state[f] + totals[pl.ds(pl.multiple_of((index * 3 + f) * 32, 32), 32), :] for f in range(3)
        )

    zero = jnp.zeros((32, ZONAL), F32)
    state = lax.fori_loop(0, pair, turn, (zero, zero, zero))
    seg = iota((8, ZONAL), 1) // 32
    chunk[...] = jnp.zeros_like(chunk)
    for x in range(2):
        state = propagate(*state)
        for f in range(3):
            held[f * 32 : (f + 1) * 32, :] = state[f]
        for f in range(3):
            packed = None
            for cr in range(4):
                piece = held[pl.ds(f * 32 + cr, 8, stride=4), :]
                piece = pltpu.roll(piece, lax.rem(32 * (cr - quarter) + ZONAL, ZONAL), 1)
                packed = piece if cr == 0 else jnp.where(seg == cr, piece, packed)
            chunk[pl.ds((2 * core + x) * 32 + f, 8, stride=4), :] = packed
        if x == 0:
            state = tuple(state[f] + jumps[f * 32 : (f + 1) * 32, :] for f in range(3))


def correct_kernel(place, fine, gathered, vectors, depths, out):
    half = place[5]
    lanes = jnp.broadcast_to(depths[...], (LAYERS, LAYERS))
    eye = iota((LAYERS, LAYERS), 0) == iota((LAYERS, LAYERS), 1)
    root = jnp.sqrt(jnp.sum(jnp.where(eye, lanes, 0.0), axis=1, keepdims=True))
    lane = iota((LAYERS, ZONAL), 1)
    for f in range(3):
        in_modes = gathered[pl.ds(half * 4 + f, LAYERS, stride=8), :]
        change = lax.dot_general(
            vectors[:, :LAYERS], in_modes, (((0,), (0,)), ((), ())),
            precision=HIGHEST, preferred_element_type=F32,
        )
        change = change * root if f == 0 else change / root
        for cr in range(4):
            spread = jnp.take_along_axis(change, cr * 32 + lane // 4, axis=1)
            for r in range(4):
                row = 4 * cr + r
                out[pl.ds(f * 256 + row, LAYERS, stride=BAND), :] = fine[f * BAND + row] + spread


def call(kernel, out_shapes, scratch=(), scalars=False, flops=1 << 20, vmem=24 << 20):
    def run(*arrays):
        vmem_spec = pl.BlockSpec(memory_space=pltpu.VMEM)
        specs = [vmem_spec] * len(arrays)
        if scalars:
            specs[0] = pl.BlockSpec(memory_space=pltpu.SMEM)
        return pl.pallas_call(
            kernel,
            out_shape=[jax.ShapeDtypeStruct(s, F32) for s in out_shapes],
            in_specs=specs,
            out_specs=[vmem_spec] * len(out_shapes),
            scratch_shapes=list(scratch),
            compiler_params=pltpu.CompilerParams(vmem_limit_bytes=vmem),
            cost_estimate=pl.CostEstimate(flops=flops, bytes_accessed=1 << 20, transcendentals=0),
        )(*arrays)

    return run


def swap(block, axes):
    return lax.all_to_all(block, axes, 0, 0, tiled=True)


def body(start_state, land_mask, fold_map, coupling, depths):
    own = start_state.reshape(3 * LAYERS * BAND, ZONAL)
    fold = fold_map.reshape(1, ZONAL)
    depth_row = depths.reshape(1, LAYERS)
    zl, x, zh, y, c = (lax.axis_index(a) for a in ("zl", "x", "zh", "y", "c"))
    position = zh * 8 + y * 2 + c
    place = jnp.stack([position, x * 4 + y, zl * 2 + c, zh, c, x // 2]).astype(jnp.int32)

    up = [(i, i + 1) for i in range(BANDS - 1)]
    down = [(b, a) for a, b in up]
    low = lax.ppermute(own, SPACE, up)
    high = lax.ppermute(own, SPACE, down)
    mask_low = lax.ppermute(land_mask, SPACE, up)
    mask_high = lax.ppermute(land_mask, SPACE, down)

    (restricted,) = call(
        restrict_kernel, [(48, ZONAL)], [pltpu.VMEM((48, 4 * ZONAL), F32)]
    )(own)
    following = lax.ppermute(restricted, TIME, [(n + 1, n) for n in range(15)])
    vectors, values = call(modes_kernel, [(LAYERS, ZONAL), (LAYERS, ZONAL)], flops=10 << 20)(
        coupling, depth_row
    )

    rows = SPAN + 2 * PAD
    state = pltpu.VMEM((rows, 2, 8, ZONAL), F32)
    table = pltpu.VMEM((rows, 8, ZONAL), F32)
    fine, chunk = call(
        fine_kernel,
        [(3 * BAND, LAYERS, ZONAL), (4 * BANDS, ZONAL)],
        [state, state, state, state, table, table, pltpu.VMEM((56, 4 * ZONAL), F32)],
        scalars=True,
    )(
        place, own, low, high, land_mask, mask_low, mask_high, fold, coupling, depth_row, vectors, following
    )

    spread = swap(chunk, PLANE)
    mine = lax.dynamic_slice_in_dim(spread, c * 64, 64, 0)
    grid = swap(jnp.concatenate([mine] * 4, axis=0), ("zh",))
    jumps, mask, total = call(
        pair_kernel, [(192, ZONAL), (32, ZONAL), (8 * 96, ZONAL)], scalars=True
    )(place, grid, values, fold)
    totals = swap(total, ("zl", "c"))
    (chunk,) = call(
        chain_kernel, [(4 * BANDS, ZONAL)], [pltpu.VMEM((96, ZONAL), F32)], scalars=True
    )(place, totals, jumps, mask, values, fold)
    change = swap(chunk, PLANE)
    (result,) = call(correct_kernel, [(3 * LAYERS * BAND, ZONAL)], scalars=True)(
        place, fine, change, vectors, depth_row
    )
    return result.reshape(1, 3, LAYERS, BAND, ZONAL)


def solution(mesh):
    parts = Mesh(mesh.devices.reshape(4, 4, 4, 4, 2), ("zl", "x", "zh", "y", "c"))
    return jax.shard_map(
        body,
        mesh=parts,
        in_specs=(P(TIME, None, None, SPACE, None), P(SPACE, None), P(), P(), P()),
        out_specs=P(TIME, None, None, SPACE, None),
        check_vma=False,
    )
```

```python
import functools

import jax
import jax.numpy as jnp
from jax import lax
from jax.experimental import pallas as pl
from jax.experimental.pallas import tpu as pltpu
from jax.sharding import Mesh
from jax.sharding import PartitionSpec as P

LAYERS = 16
ZONAL = 128
FINE_STEPS = 8
BAND = 16
BANDS = 32
EXTENT = BAND * BANDS
HALO = 2 * FINE_STEPS
SPAN = BAND + 2 * HALO
FRICTION = 0.02
CUT = 2 * LAYERS * BAND
MASK = 3 * LAYERS * BAND
HIGHEST = lax.Precision.HIGHEST
F32 = jnp.float32
BF16 = jnp.bfloat16

SPACE = ("zh", "y", "c")
TIME = ("zl", "x")
PLANE = ("x", "y", "c")

SHIFT = 1.0


def iota(shape, axis):
    return lax.broadcasted_iota(jnp.int32, shape, axis)


def two_parts(x):
    top = x.astype(BF16)
    return top, (x - top.astype(F32)).astype(BF16)


def dot3(a, b):
    (a_top, a_rest), (b_top, b_rest) = two_parts(a), two_parts(b)
    left = jnp.concatenate([a_top, a_top, a_rest], axis=1)
    right = jnp.concatenate([b_top, b_rest, b_top], axis=0)
    return jnp.dot(left, right, preferred_element_type=F32)


def block_mean(rows):
    part = iota(rows[0].shape, 1) % 4

    def pairs(x, y, step):
        first = (part & step) == 0
        return jnp.where(first, x + pltpu.roll(x, ZONAL - step, 1), y + pltpu.roll(y, step, 1))

    return pairs(pairs(rows[0], rows[1], 1), pairs(rows[2], rows[3], 1), 2) * (1.0 / 16.0)


def pack_kernel(state, mask, packed, first, rest, restricted, rows, sems):
    copies = [
        pltpu.make_async_copy(state, packed.at[pl.ds(0, MASK)], sems.at[0]),
        pltpu.make_async_copy(mask, rows, sems.at[1]),
    ]
    for copy in copies:
        copy.start()
    for copy in copies:
        copy.wait()
    packed[MASK:, :] = rows[...].astype(F32)
    first[...] = packed[:CUT, :]
    rest[...] = packed[CUT:, :]
    for f in range(3):
        rows = []
        for cr in range(4):
            here = [packed[pl.ds(f * 256 + 4 * cr + r, LAYERS, stride=BAND), :] for r in range(4)]
            rows.append(here[0] + here[1] + here[2] + here[3])
        restricted[f * LAYERS : (f + 1) * LAYERS, :] = block_mean(rows)


def modes_kernel(coupling, depths, vectors, values):
    row = iota((LAYERS, ZONAL), 0)
    lane = iota((LAYERS, ZONAL), 1)
    eye = row == lane
    root = jnp.sqrt(depths[...])
    root = jnp.concatenate([root, jnp.zeros((1, ZONAL - LAYERS), F32)], axis=1)
    root_lanes = jnp.broadcast_to(root, (LAYERS, ZONAL))
    root_rows = jnp.sum(jnp.where(eye, root_lanes, 0.0), axis=1, keepdims=True)
    matrix = jnp.concatenate([coupling[...], jnp.zeros((LAYERS, ZONAL - LAYERS), F32)], axis=1)
    matrix = matrix * root_lanes * root_rows
    start = matrix + jnp.where(eye, SHIFT, 0.0) + jnp.where(lane == row + LAYERS, 1.0, 0.0)
    active = iota((8, ZONAL), 1) < LAYERS
    sub = iota((8, ZONAL), 0)

    def sums(x):
        return jnp.broadcast_to(jnp.sum(jnp.where(active, x, 0.0), axis=1, keepdims=True), x.shape)

    def turn(width, x):
        if width == 8:
            return pltpu.roll(x, 1, 0)
        return jnp.where((sub & (width - 1)) == 0, pltpu.roll(x, 9 - width, 0), pltpu.roll(x, 1, 0))

    def regroup(half, x, y):
        low = (sub & half) == 0
        return jnp.where(low, x, pltpu.roll(y, half, 0)), jnp.where(low, pltpu.roll(x, 8 - half, 0), y)

    def sweep(carry):
        count, _, x, y = carry
        xx, yy = sums(x * x), sums(y * y)
        worst = jnp.zeros((8, ZONAL), F32)
        for width in (8, 4, 2, 1):
            for _ in range(width):
                xy = sums(x * y)
                gap = yy - xx
                side = jnp.maximum(jnp.abs(gap), 1e-12)
                scale = lax.rsqrt(side * side + 4.0 * xy * xy)
                square = 0.5 + 0.5 * side * scale
                cosine_over = lax.rsqrt(square)
                signed = jnp.where(gap >= 0.0, xy, -xy) * scale
                cosine = square * cosine_over
                sine = signed * cosine_over
                tangent_xy = signed * xy / square
                worst = jnp.maximum(worst, jnp.abs(xy))
                x, y = cosine * x - sine * y, sine * x + cosine * y
                xx, yy = xx - tangent_xy, yy + tangent_xy
                if width > 1:
                    y, yy = turn(width, y), turn(width, yy)
            if width > 1:
                x, y = regroup(width // 2, x, y)
                xx, yy = regroup(width // 2, xx, yy)
        return count + 1, jnp.max(worst), x, y

    def unfinished(carry):
        return jnp.logical_and(carry[0] < 12, carry[1] > 2e-4)

    _, _, x, y = lax.while_loop(unfinished, sweep, (0, jnp.float32(1.0), start[:8], start[8:]))
    x = jnp.concatenate([x, y], axis=0)
    active = lane < LAYERS
    turned = pltpu.roll(x, ZONAL - LAYERS, 1)
    vectors[...] = jnp.where(active, turned, 0.0)
    value = jnp.sum(jnp.where(active, x * turned, 0.0), axis=1, keepdims=True) - SHIFT
    values[...] = jnp.broadcast_to(value, (LAYERS, ZONAL))


def east(x):
    flat = x.reshape(-1, ZONAL)
    return (pltpu.roll(flat, ZONAL - 1, 1) - pltpu.roll(flat, 1, 1)).reshape(x.shape)


def fine_tools(fields, ps, ms, fs, coupling, depths):
    hs, us, vs = fields
    half_top, half_rest = two_parts(0.5 * coupling[...])
    weights = jnp.concatenate([half_top, half_top, half_rest], axis=1)
    lanes = jnp.broadcast_to(depths[...], (LAYERS, LAYERS))
    eye = iota((LAYERS, LAYERS), 0) == iota((LAYERS, LAYERS), 1)
    thick = 0.5 * jnp.sum(jnp.where(eye, lanes, 0.0), axis=1, keepdims=True)
    thick = jnp.broadcast_to(thick, (LAYERS, ZONAL)).reshape(1, 2, 8, ZONAL)
    keep = 1.0 - FRICTION

    def pressure(low, high):
        wide = jnp.concatenate([hs[j].reshape(LAYERS, ZONAL) for j in range(low, high)], axis=1)
        top, rest = two_parts(wide)
        stacked = jnp.concatenate([top, rest, top], axis=0)
        result = jnp.dot(weights, stacked, preferred_element_type=F32)
        for j in range(low, high):
            ps[j] = result[:, (j - low) * ZONAL : (j - low + 1) * ZONAL].reshape(2, 8, ZONAL)

    def velocity(low, high):
        m = ms[low:high][:, None]
        f = fs[low:high][:, None]
        u = us[low:high]
        v = vs[low:high]
        u = m * (keep * u + f * v - east(ps[low:high]))
        v = m * (keep * v - f * u - (ps[low + 1 : high + 1] - ps[low - 1 : high - 1]))
        us[low:high] = u
        vs[low:high] = v

    def thickness(low, high):
        m = ms[low:high][:, None]
        spread = east(us[low:high]) + (vs[low + 1 : high + 1] - vs[low - 1 : high - 1])
        hs[low:high] = m * (hs[low:high] - thick * spread)

    def steps(bounds):
        for low, ends in bounds:
            for at in range(low, ends[0], 4):
                pressure(at, min(at + 4, ends[0]))
            for at in range(low + 1, ends[1], 4):
                velocity(at, min(at + 4, ends[1]))
            for at in range(low + 2, ends[2], 4):
                thickness(at, min(at + 4, ends[2]))

    return steps


def core_index():
    return lax.axis_index("c")


def band_index():
    return lax.axis_index("zh") * 8 + lax.axis_index("y") * 2 + lax.axis_index("c")


def mode_index():
    return lax.axis_index("x") * 4 + lax.axis_index("y")


def put_band(fields, ms, begin, blocks, cut, core, sign):
    for odd in (False, True):

        @pl.when(core == int(odd))
        def _():
            for r in range(BAND):
                row = begin + (BAND - 1 - r if odd else r)
                for f in range(3):
                    at = f * 256 + r - (cut if f == 2 else 0)
                    value = blocks[f // 2][pl.ds(at, LAYERS, stride=BAND), :].reshape(2, 8, ZONAL)
                    fields[f][row] = sign * value if f == 2 else value
                at = MASK - cut + r
                ms[row] = jnp.broadcast_to(blocks[1][at : at + 1, :], (8, ZONAL))


def coriolis_table(fs, position, core, sign):
    offset = iota(fs.shape, 0) - HALO
    rows = position * BAND + jnp.where(core == 1, BAND - 1 - offset, offset)
    latitude = (rows.astype(F32) + 0.5) / float(EXTENT)
    latitude = jnp.where(latitude > 1.0, 2.0 - latitude, latitude)
    fs[...] = sign * (0.3 * (latitude - 0.5))


KEPT = 20


def inner_kernel(
    own, mate_first, mate_rest, fold, coupling, depths, h_out, u_out, v_out, fold_out, hs, us, vs, ps, ms, fs
):
    core = core_index()
    sign = (1 - 2 * core).astype(F32)
    fields = (hs, us, vs)
    put_band(fields, ms, HALO, (own, own), 0, core, sign)
    put_band(fields, ms, HALO + BAND, (mate_first, mate_rest), CUT, core, sign)
    coriolis_table(fs, band_index(), core, sign)
    steps = fine_tools(fields, ps, ms, fs, coupling, depths)
    ends = [SPAN - 2 * t for t in range(FINE_STEPS)]
    steps([(HALO + 2 * t, (ends[t], ends[t] - 1, ends[t] - 2)) for t in range(FINE_STEPS)])
    fold_out[...] = fold[...].astype(F32)
    for out, field in zip((h_out, u_out, v_out), fields):
        out[...] = field[HALO : HALO + KEPT]


def outer_kernel(
    own, other, h_in, u_in, v_in, fold, coupling, depths, vectors, following,
    fine, chunk, hs, us, vs, ps, ms, fs,
):
    position = band_index()
    core = core_index()
    sign = (1 - 2 * core).astype(F32)
    on_top = position == BANDS - 1
    fields = (hs, us, vs)
    for field, kept in zip(fields, (h_in, u_in, v_in)):
        field[HALO : HALO + KEPT] = kept[...]
    for r in range(BAND):
        row = HALO + r + core * (BAND - 1 - 2 * r)
        ms[row] = jnp.broadcast_to(own[MASK + r : MASK + r + 1, :], (8, ZONAL))

    @pl.when(jnp.logical_not(on_top))
    def _():
        put_band(fields, ms, 0, (other, other), 0, core, sign)

    @pl.when(on_top)
    def _():
        index = jnp.broadcast_to(fold[...].astype(jnp.int32), (LAYERS, ZONAL))
        for r in range(BAND):
            for f in range(3):
                image = own[pl.ds(f * 256 + r, LAYERS, stride=BAND), :]
                image = jnp.take_along_axis(image, index, axis=1).reshape(2, 8, ZONAL)
                fields[f][r] = -image if f == 1 else image
            image = jnp.broadcast_to(own[MASK + r : MASK + r + 1, :], (8, ZONAL))
            ms[r] = jnp.take_along_axis(image, index[:8], axis=1)

    coriolis_table(fs, position, core, sign)
    steps = fine_tools(fields, ps, ms, fs, coupling, depths)
    steps([(2 * t, (2 * t + 18, 2 * t + 17, 2 * t + 18)) for t in range(FINE_STEPS)])

    def row_of(r):
        return HALO + r + core * (BAND - 1 - 2 * r)

    root = jnp.sqrt(depths[...])
    jumps = []
    for f in range(3):
        rows = []
        for cr in range(4):
            here = [fields[f][row_of(4 * cr + r)].reshape(LAYERS, ZONAL) for r in range(4)]
            if f == 2:
                here = [sign * row for row in here]
            for r in range(4):
                fine[f * BAND + 4 * cr + r] = here[r]
            rows.append(here[0] + here[1] + here[2] + here[3])
        jumps.append(block_mean(rows) - following[f * LAYERS : (f + 1) * LAYERS, :])
    of_thickness = dot3(vectors[:, :LAYERS] / root, jumps[0])
    of_velocity = dot3(vectors[:, :LAYERS] * root, jnp.concatenate(jumps[1:], axis=1))
    for f, in_modes in enumerate((of_thickness, of_velocity[:, :ZONAL], of_velocity[:, ZONAL:])):
        chunk[pl.ds(f, LAYERS, stride=8), :] = in_modes
        chunk[pl.ds(4 + f, LAYERS, stride=8), :] = in_modes
    rows = []
    for cr in range(4):
        here = [ms[row_of(4 * cr + r)] for r in range(4)]
        rows.append(here[0] + here[1] + here[2] + here[3])
    chunk[pl.ds(3, BANDS, stride=4), :] = jnp.broadcast_to(block_mean(rows)[:1], (BANDS, ZONAL))


def coarse_tools(value, masks, fold):
    sub = iota((8, ZONAL), 0)
    lane = iota((8, ZONAL), 1)
    seg = lane % 4
    coriolis = []
    for cr in range(4):
        position = ((seg * 8 + sub) * 4 + cr).astype(F32)
        coriolis.append((4.0 * 0.3) * ((position + 0.5) / float(EXTENT // 4) - 0.5))
    keep = 1.0 - 4.0 * FRICTION
    k = fold[0, 0] // 4
    fold_index = 4 * ((k - lane // 4 + 32) % 32) + 3
    last, top = sub == 7, jnp.logical_and(sub == 7, seg == 3)
    first, bottom = sub == 0, jnp.logical_and(sub == 0, seg == 0)

    def east(x):
        return pltpu.roll(x, ZONAL - 4, 1) - pltpu.roll(x, 4, 1)

    def north(x, sign):
        up = pltpu.roll(x[0], 7, 0)
        up = jnp.where(last, pltpu.roll(up, ZONAL - 1, 1), up)
        up = jnp.where(top, sign * jnp.take_along_axis(x[3], fold_index, axis=1), up)
        down = pltpu.roll(x[3], 1, 0)
        down = jnp.where(first, pltpu.roll(down, 1, 1), down)
        down = jnp.where(bottom, 0.0, down)
        return [x[1] - down, x[2] - x[0], x[3] - x[1], up - x[2]]

    def propagate(state):
        h, u, v = state
        for _ in range(2):
            p = [(0.5 * value) * x for x in h]
            north_p = north(p, 1.0)
            u = [masks[i] * (keep * u[i] + coriolis[i] * v[i] - east(p[i])) for i in range(4)]
            v = [masks[i] * (keep * v[i] - coriolis[i] * u[i] - north_p[i]) for i in range(4)]
            north_v = north(v, -1.0)
            h = [masks[i] * (h[i] - 0.5 * (east(u[i]) + north_v[i])) for i in range(4)]
        return [h, u, v]

    return propagate


def load_state(ref, begin=0):
    return [[ref[begin + f * 32 + cr * 8 : begin + f * 32 + cr * 8 + 8, :] for cr in range(4)] for f in range(3)]


def store_state(ref, state, begin=0):
    for f in range(3):
        for cr in range(4):
            ref[begin + f * 32 + cr * 8 : begin + f * 32 + cr * 8 + 8, :] = state[f][cr]


def add_state(a, b):
    return [[x + y for x, y in zip(p, q)] for p, q in zip(a, b)]


def load_masks(ref):
    return [ref[cr * 8 : cr * 8 + 8, :] for cr in range(4)]


def pair_kernel(gathered, values, fold, jumps, mask_out, total):
    lane = iota((8, ZONAL), 1)
    seg = lane % 4
    for x in range(2):
        for f in range(4 if x == 0 else 3):
            rows = [None] * 4
            for zh in range(4):
                piece = gathered[pl.ds(zh * 64 + x * 32 + f, 8, stride=4), :]
                for cr in range(4):
                    shift = (zh - cr) % ZONAL
                    moved = pltpu.roll(piece, shift, 1) if shift else piece
                    rows[cr] = moved if zh == 0 else jnp.where(seg == zh, moved, rows[cr])
            for cr in range(4):
                if f == 3:
                    mask_out[cr * 8 : cr * 8 + 8, :] = rows[cr]
                else:
                    begin = x * 96 + f * 32 + cr * 8
                    jumps[begin : begin + 8, :] = rows[cr]
    propagate = coarse_tools(values[pl.ds(mode_index(), 1), :], load_masks(mask_out), fold)
    store_state(total, add_state(propagate(load_state(jumps)), load_state(jumps, 96)))


def group_kernel(total, mate, mask, values, fold, both):
    propagate = coarse_tools(values[pl.ds(mode_index(), 1), :], load_masks(mask), fold)
    odd = core_index() == 1
    mine, theirs = load_state(total), load_state(mate)
    earlier = [[jnp.where(odd, t, m) for m, t in zip(a, b)] for a, b in zip(mine, theirs)]
    later = [[jnp.where(odd, m, t) for m, t in zip(a, b)] for a, b in zip(mine, theirs)]
    store_state(both, add_state(propagate(propagate(earlier)), later))


def chain_kernel(one, two, three, mate, jumps, mask, values, fold, chunk):
    quarter = lax.axis_index("zh")
    core = core_index()
    propagate = coarse_tools(values[pl.ds(mode_index(), 1), :], load_masks(mask), fold)

    def twice(state):
        return propagate(propagate(state))

    state = load_state(three)
    for ref in (two, one):
        state = lax.fori_loop(0, 2, lambda _, s: twice(s), state)
        state = add_state(state, load_state(ref))
    state = lax.fori_loop(0, core, lambda _, s: add_state(twice(s), load_state(mate)), state)
    seg = iota((8, ZONAL), 1) % 4
    chunk[...] = jnp.zeros_like(chunk)
    for x in range(2):
        state = propagate(state)
        for f in range(3):
            packed = None
            for cr in range(4):
                piece = pltpu.roll(state[f][cr], lax.rem(cr - quarter + ZONAL, ZONAL), 1)
                packed = piece if cr == 0 else jnp.where(seg == cr, piece, packed)
            chunk[pl.ds((2 * core + x) * 32 + f, 8, stride=4), :] = packed
        if x == 0:
            state = add_state(state, load_state(jumps))


def correct_kernel(fine, gathered, vectors, depths, out, result, sems):
    half = lax.axis_index("x") // 2
    lanes = jnp.broadcast_to(depths[...], (LAYERS, LAYERS))
    eye = iota((LAYERS, LAYERS), 0) == iota((LAYERS, LAYERS), 1)
    root = jnp.sqrt(jnp.sum(jnp.where(eye, lanes, 0.0), axis=1, keepdims=True))
    lane = iota((LAYERS, ZONAL), 1)
    copies = []
    for f in range(3):
        in_modes = gathered[pl.ds(half * 4 + f, LAYERS, stride=8), :]
        change = lax.dot_general(
            vectors[:, :LAYERS], in_modes, (((0,), (0,)), ((), ())),
            precision=HIGHEST, preferred_element_type=F32,
        )
        change = change * root if f == 0 else change / root
        for cr in range(4):
            spread = jnp.take_along_axis(change, lane // 4 * 4 + cr, axis=1)
            for r in range(4):
                row = 4 * cr + r
                result[pl.ds(f * 256 + row, LAYERS, stride=BAND), :] = fine[f * BAND + row] + spread
        here = pl.ds(f * 256, 256)
        copies.append(pltpu.make_async_copy(result.at[here], out.at[here], sems.at[f]))
        copies[-1].start()
    for copy in copies:
        copy.wait()


def call(kernel, out_shapes, scratch=(), spaces=None, out_space=pltpu.VMEM, flops=1 << 20, vmem=24 << 20):
    def run(*arrays):
        specs = [pl.BlockSpec(memory_space=s) for s in spaces or (pltpu.VMEM,) * len(arrays)]
        return pl.pallas_call(
            kernel,
            out_shape=[jax.ShapeDtypeStruct(s, F32) for s in out_shapes],
            in_specs=specs,
            out_specs=[pl.BlockSpec(memory_space=out_space)] * len(out_shapes),
            scratch_shapes=list(scratch),
            compiler_params=pltpu.CompilerParams(vmem_limit_bytes=vmem),
            cost_estimate=pl.CostEstimate(flops=flops, bytes_accessed=1 << 20, transcendentals=0),
        )(*arrays)

    return run


def swap(block, axes):
    return lax.all_to_all(block, axes, 0, 0, tiled=True)


def body(start_state, land_mask, fold_map, coupling, depths):
    own, first, rest, restricted = call(
        pack_kernel,
        [(MASK + BAND, ZONAL), (CUT, ZONAL), (MASK + BAND - CUT, ZONAL), (3 * LAYERS, ZONAL)],
        [pltpu.VMEM((BAND, ZONAL), jnp.int32), pltpu.SemaphoreType.DMA((2,))],
        spaces=(pl.ANY, pl.ANY),
    )(start_state.reshape(MASK, ZONAL), land_mask)
    fold = fold_map.reshape(1, ZONAL)
    depth_row = depths.reshape(1, LAYERS)
    across = [(i, i + 1) for i in range(1, BANDS - 1, 2)]
    across += [(b, a) for a, b in across]
    other = lax.ppermute(own, SPACE, across)
    following = lax.ppermute(restricted, TIME, [(n + 1, n) for n in range(15)])
    vectors, values = call(modes_kernel, [(LAYERS, ZONAL), (LAYERS, ZONAL)], flops=10 << 20)(
        coupling, depth_row
    )
    inside = [(i, i ^ 1) for i in range(BANDS)]
    mate = [lax.ppermute(part, SPACE, inside) for part in (first, rest)]

    state = pltpu.VMEM((SPAN, 2, 8, ZONAL), F32)
    table = pltpu.VMEM((SPAN, 8, ZONAL), F32)
    scratch = [state, state, state, state, table, table]
    *inner, fold_held = call(
        inner_kernel, [(KEPT, 2, 8, ZONAL)] * 3 + [(1, ZONAL)], scratch, flops=4 << 20
    )(own, *mate, fold, coupling, depth_row)
    fine, chunk = call(
        outer_kernel, [(3 * BAND, LAYERS, ZONAL), (4 * BANDS, ZONAL)], scratch
    )(
        own, other, *inner, fold_held, coupling, depth_row, vectors, following
    )

    spread = swap(chunk, PLANE)
    mine = lax.dynamic_slice_in_dim(spread, lax.axis_index("c") * 64, 64, 0)
    grid = swap(jnp.concatenate([mine] * 4, axis=0), ("zh",))
    jumps, mask, total = call(
        pair_kernel, [(192, ZONAL), (32, ZONAL), (96, ZONAL)]
    )(grid, values, fold)
    mate = lax.ppermute(total, ("c",), [(0, 1), (1, 0)])
    (both,) = call(group_kernel, [(96, ZONAL)])(total, mate, mask, values, fold)
    one, two, three = (
        lax.ppermute(both, ("zl",), [(i, i + d) for i in range(4 - d)]) for d in (1, 2, 3)
    )
    (chunk,) = call(chain_kernel, [(4 * BANDS, ZONAL)])(
        one, two, three, mate, jumps, mask, values, fold
    )
    change = swap(chunk, PLANE)
    (result,) = call(
        correct_kernel,
        [(MASK, ZONAL)],
        [pltpu.VMEM((MASK, ZONAL), F32), pltpu.SemaphoreType.DMA((3,))],
        out_space=pl.ANY,
    )(
        fine, change, vectors, depth_row
    )
    return result.reshape(1, 3, LAYERS, BAND, ZONAL)


def solution(mesh):
    parts = Mesh(mesh.devices.reshape(4, 4, 4, 4, 2), ("zl", "x", "zh", "y", "c"))
    return jax.shard_map(
        body,
        mesh=parts,
        in_specs=(P(TIME, None, None, SPACE, None), P(SPACE, None), P(), P(), P()),
        out_specs=P(TIME, None, None, SPACE, None),
        check_vma=False,
    )
```

```python
import functools

import jax
import jax.numpy as jnp
from jax import lax
from jax.experimental import pallas as pl
from jax.experimental.pallas import tpu as pltpu
from jax.sharding import Mesh
from jax.sharding import PartitionSpec as P

LAYERS = 16
ZONAL = 128
FINE_STEPS = 8
BAND = 16
BANDS = 32
EXTENT = BAND * BANDS
HALO = 2 * FINE_STEPS
SPAN = BAND + 2 * HALO
FRICTION = 0.02
CUT = 2 * LAYERS * BAND
MASK = 3 * LAYERS * BAND
HIGHEST = lax.Precision.HIGHEST
F32 = jnp.float32
BF16 = jnp.bfloat16

SPACE = ("zh", "y", "c")
TIME = ("zl", "x")
PLANE = ("x", "y", "c")

SHIFT = 1.0


def iota(shape, axis):
    return lax.broadcasted_iota(jnp.int32, shape, axis)


def two_parts(x):
    top = x.astype(BF16)
    return top, (x - top.astype(F32)).astype(BF16)


def dot3(a, b):
    (a_top, a_rest), (b_top, b_rest) = two_parts(a), two_parts(b)
    left = jnp.concatenate([a_top, a_top, a_rest], axis=1)
    right = jnp.concatenate([b_top, b_rest, b_top], axis=0)
    return jnp.dot(left, right, preferred_element_type=F32)


def block_mean(rows):
    part = iota(rows[0].shape, 1) % 4

    def pairs(x, y, step):
        first = (part & step) == 0
        return jnp.where(first, x + pltpu.roll(x, ZONAL - step, 1), y + pltpu.roll(y, step, 1))

    return pairs(pairs(rows[0], rows[1], 1), pairs(rows[2], rows[3], 1), 2) * (1.0 / 16.0)


VELOCITY_AT = (0, LAYERS * BAND, LAYERS * (2 * BAND - 1))
MASK_AT = LAYERS * (3 * BAND - 2)


def pack_kernel(state, mask, sent, first, rest, restricted, rows, sems):
    copies = [
        pltpu.make_async_copy(state.at[pl.ds(0, CUT)], first, sems.at[0]),
        pltpu.make_async_copy(state.at[pl.ds(CUT, MASK - CUT)], rest.at[pl.ds(0, MASK - CUT)], sems.at[1]),
        pltpu.make_async_copy(mask, rows, sems.at[2]),
    ]
    for copy in copies:
        copy.start()
    for copy in copies:
        copy.wait()
    rest[MASK - CUT :, :] = rows[...].astype(F32)

    def row_of(f, r):
        if f < 2:
            return first[pl.ds(f * 256 + r, LAYERS, stride=BAND), :]
        return rest[pl.ds(r, LAYERS, stride=BAND), :]

    for odd in (False, True):

        @pl.when(core_index() == int(odd))
        def _():
            for k in range(BAND):
                r = BAND - 1 - k if odd else k
                for f in range(3 if k < BAND - 1 else 1):
                    at = VELOCITY_AT[f] + LAYERS * k
                    sent[at : at + LAYERS, :] = row_of(f, r)
                sent[MASK_AT + k : MASK_AT + k + 1, :] = rest[MASK - CUT + r : MASK - CUT + r + 1, :]

    for f in range(3):
        rows = []
        for cr in range(4):
            here = [row_of(f, 4 * cr + r) for r in range(4)]
            rows.append(here[0] + here[1] + here[2] + here[3])
        restricted[f * LAYERS : (f + 1) * LAYERS, :] = block_mean(rows)


def modes_kernel(coupling, depths, vectors, values):
    row = iota((LAYERS, ZONAL), 0)
    lane = iota((LAYERS, ZONAL), 1)
    eye = row == lane
    root = jnp.sqrt(depths[...])
    root = jnp.concatenate([root, jnp.zeros((1, ZONAL - LAYERS), F32)], axis=1)
    root_lanes = jnp.broadcast_to(root, (LAYERS, ZONAL))
    root_rows = jnp.sum(jnp.where(eye, root_lanes, 0.0), axis=1, keepdims=True)
    matrix = jnp.concatenate([coupling[...], jnp.zeros((LAYERS, ZONAL - LAYERS), F32)], axis=1)
    matrix = matrix * root_lanes * root_rows
    start = matrix + jnp.where(eye, SHIFT, 0.0) + jnp.where(lane == row + LAYERS, 1.0, 0.0)
    active = iota((8, ZONAL), 1) < LAYERS
    sub = iota((8, ZONAL), 0)

    def sums(x):
        return jnp.broadcast_to(jnp.sum(jnp.where(active, x, 0.0), axis=1, keepdims=True), x.shape)

    def turn(width, x):
        if width == 8:
            return pltpu.roll(x, 1, 0)
        return jnp.where((sub & (width - 1)) == 0, pltpu.roll(x, 9 - width, 0), pltpu.roll(x, 1, 0))

    def regroup(half, x, y):
        low = (sub & half) == 0
        return jnp.where(low, x, pltpu.roll(y, half, 0)), jnp.where(low, pltpu.roll(x, 8 - half, 0), y)

    def sweep(carry):
        count, _, x, y = carry
        xx, yy = sums(x * x), sums(y * y)
        worst = jnp.zeros((8, ZONAL), F32)
        for width in (8, 4, 2, 1):
            for _ in range(width):
                xy = sums(x * y)
                gap = yy - xx
                side = jnp.maximum(jnp.abs(gap), 1e-12)
                scale = lax.rsqrt(side * side + 4.0 * xy * xy)
                square = 0.5 + 0.5 * side * scale
                cosine_over = lax.rsqrt(square)
                signed = jnp.where(gap >= 0.0, xy, -xy) * scale
                cosine = square * cosine_over
                sine = signed * cosine_over
                tangent_xy = signed * xy / square
                worst = jnp.maximum(worst, jnp.abs(xy))
                x, y = cosine * x - sine * y, sine * x + cosine * y
                xx, yy = xx - tangent_xy, yy + tangent_xy
                if width > 1:
                    y, yy = turn(width, y), turn(width, yy)
            if width > 1:
                x, y = regroup(width // 2, x, y)
                xx, yy = regroup(width // 2, xx, yy)
        return count + 1, jnp.max(worst), x, y

    def unfinished(carry):
        return jnp.logical_and(carry[0] < 12, carry[1] > 2e-4)

    _, _, x, y = lax.while_loop(unfinished, sweep, (0, jnp.float32(1.0), start[:8], start[8:]))
    x = jnp.concatenate([x, y], axis=0)
    active = lane < LAYERS
    turned = pltpu.roll(x, ZONAL - LAYERS, 1)
    vectors[...] = jnp.where(active, turned, 0.0)
    value = jnp.sum(jnp.where(active, x * turned, 0.0), axis=1, keepdims=True) - SHIFT
    values[...] = jnp.broadcast_to(value, (LAYERS, ZONAL))


def east(x):
    flat = x.reshape(-1, ZONAL)
    return (pltpu.roll(flat, ZONAL - 1, 1) - pltpu.roll(flat, 1, 1)).reshape(x.shape)


def fine_tools(fields, ps, ms, fs, coupling, depths):
    hs, us, vs = fields
    half_top, half_rest = two_parts(0.5 * coupling[...])
    weights = jnp.concatenate([half_top, half_top, half_rest], axis=1)
    lanes = jnp.broadcast_to(depths[...], (LAYERS, LAYERS))
    eye = iota((LAYERS, LAYERS), 0) == iota((LAYERS, LAYERS), 1)
    thick = 0.5 * jnp.sum(jnp.where(eye, lanes, 0.0), axis=1, keepdims=True)
    thick = jnp.broadcast_to(thick, (LAYERS, ZONAL)).reshape(1, 2, 8, ZONAL)
    keep = 1.0 - FRICTION

    def pressure(low, high):
        wide = jnp.concatenate([hs[j].reshape(LAYERS, ZONAL) for j in range(low, high)], axis=1)
        top, rest = two_parts(wide)
        stacked = jnp.concatenate([top, rest, top], axis=0)
        result = jnp.dot(weights, stacked, preferred_element_type=F32)
        for j in range(low, high):
            ps[j] = result[:, (j - low) * ZONAL : (j - low + 1) * ZONAL].reshape(2, 8, ZONAL)

    def velocity(low, high):
        m = ms[low:high][:, None]
        f = fs[low:high][:, None]
        u = us[low:high]
        v = vs[low:high]
        u = m * (keep * u + f * v - east(ps[low:high]))
        v = m * (keep * v - f * u - (ps[low + 1 : high + 1] - ps[low - 1 : high - 1]))
        us[low:high] = u
        vs[low:high] = v

    def thickness(low, high):
        m = ms[low:high][:, None]
        spread = east(us[low:high]) + (vs[low + 1 : high + 1] - vs[low - 1 : high - 1])
        hs[low:high] = m * (hs[low:high] - thick * spread)

    def steps(bounds):
        for low, ends in bounds:
            for at in range(low, ends[0], 4):
                pressure(at, min(at + 4, ends[0]))
            for at in range(low + 1, ends[1], 4):
                velocity(at, min(at + 4, ends[1]))
            for at in range(low + 2, ends[2], 4):
                thickness(at, min(at + 4, ends[2]))

    return steps


def core_index():
    return lax.axis_index("c")


def band_index():
    return lax.axis_index("zh") * 8 + lax.axis_index("y") * 2 + lax.axis_index("c")


def mode_index():
    return lax.axis_index("x") * 4 + lax.axis_index("y")


def put_band(fields, ms, begin, blocks, core, sign):
    for odd in (False, True):

        @pl.when(core == int(odd))
        def _():
            for r in range(BAND):
                row = begin + (BAND - 1 - r if odd else r)
                for f in range(3):
                    at = f * 256 + r - (CUT if f == 2 else 0)
                    value = blocks[f // 2][pl.ds(at, LAYERS, stride=BAND), :].reshape(2, 8, ZONAL)
                    fields[f][row] = sign * value if f == 2 else value
                at = MASK - CUT + r
                ms[row] = jnp.broadcast_to(blocks[1][at : at + 1, :], (8, ZONAL))


def coriolis_table(fs, position, core, sign):
    offset = iota(fs.shape, 0) - HALO
    rows = position * BAND + jnp.where(core == 1, BAND - 1 - offset, offset)
    latitude = (rows.astype(F32) + 0.5) / float(EXTENT)
    latitude = jnp.where(latitude > 1.0, 2.0 - latitude, latitude)
    fs[...] = sign * (0.3 * (latitude - 0.5))


KEPT = 20


def inner_kernel(
    own_first, own_rest, mate_first, mate_rest, fold, coupling, depths, h_out, u_out, v_out, fold_out, hs, us, vs, ps, ms, fs
):
    core = core_index()
    sign = (1 - 2 * core).astype(F32)
    fields = (hs, us, vs)
    put_band(fields, ms, HALO, (own_first, own_rest), core, sign)
    put_band(fields, ms, HALO + BAND, (mate_first, mate_rest), core, sign)
    coriolis_table(fs, band_index(), core, sign)
    steps = fine_tools(fields, ps, ms, fs, coupling, depths)
    ends = [SPAN - 2 * t for t in range(FINE_STEPS)]
    steps([(HALO + 2 * t, (ends[t], ends[t] - 1, ends[t] - 2)) for t in range(FINE_STEPS)])
    fold_out[...] = fold[...].astype(F32)
    for out, field in zip((h_out, u_out, v_out), fields):
        out[...] = field[HALO : HALO + KEPT]


def outer_kernel(
    own_first, own_rest, other, h_in, u_in, v_in, fold, coupling, depths, vectors, following,
    fine, chunk, hs, us, vs, ps, ms, fs,
):
    position = band_index()
    core = core_index()
    sign = (1 - 2 * core).astype(F32)
    on_top = position == BANDS - 1
    fields = (hs, us, vs)
    for field, kept in zip(fields, (h_in, u_in, v_in)):
        field[HALO : HALO + KEPT] = kept[...]
    for r in range(BAND):
        row = HALO + r + core * (BAND - 1 - 2 * r)
        ms[row] = jnp.broadcast_to(own_rest[MASK - CUT + r : MASK - CUT + r + 1, :], (8, ZONAL))

    @pl.when(jnp.logical_not(on_top))
    def _():
        for k in range(BAND):
            for f in range(3 if k < BAND - 1 else 1):
                at = VELOCITY_AT[f] + LAYERS * k
                value = other[at : at + LAYERS, :].reshape(2, 8, ZONAL)
                fields[f][BAND - 1 - k] = sign * value if f == 2 else value
            ms[BAND - 1 - k] = jnp.broadcast_to(other[MASK_AT + k : MASK_AT + k + 1, :], (8, ZONAL))

    @pl.when(on_top)
    def _():
        index = jnp.broadcast_to(fold[...].astype(jnp.int32), (LAYERS, ZONAL))
        for r in range(BAND):
            for f in range(3):
                block, at = (own_first, f * 256 + r) if f < 2 else (own_rest, r)
                image = block[pl.ds(at, LAYERS, stride=BAND), :]
                image = jnp.take_along_axis(image, index, axis=1).reshape(2, 8, ZONAL)
                fields[f][r] = -image if f == 1 else image
            image = jnp.broadcast_to(own_rest[MASK - CUT + r : MASK - CUT + r + 1, :], (8, ZONAL))
            ms[r] = jnp.take_along_axis(image, index[:8], axis=1)

    coriolis_table(fs, position, core, sign)
    steps = fine_tools(fields, ps, ms, fs, coupling, depths)
    steps([(2 * t, (2 * t + 18, 2 * t + 17, 2 * t + 18)) for t in range(FINE_STEPS)])

    def row_of(r):
        return HALO + r + core * (BAND - 1 - 2 * r)

    root = jnp.sqrt(depths[...])
    jumps = []
    for f in range(3):
        rows = []
        for cr in range(4):
            here = [fields[f][row_of(4 * cr + r)].reshape(LAYERS, ZONAL) for r in range(4)]
            if f == 2:
                here = [sign * row for row in here]
            for r in range(4):
                fine[f * BAND + 4 * cr + r] = here[r]
            rows.append(here[0] + here[1] + here[2] + here[3])
        jumps.append(block_mean(rows) - following[f * LAYERS : (f + 1) * LAYERS, :])
    of_thickness = dot3(vectors[:, :LAYERS] / root, jumps[0])
    of_velocity = dot3(vectors[:, :LAYERS] * root, jnp.concatenate(jumps[1:], axis=1))
    for f, in_modes in enumerate((of_thickness, of_velocity[:, :ZONAL], of_velocity[:, ZONAL:])):
        chunk[pl.ds(f, LAYERS, stride=8), :] = in_modes
        chunk[pl.ds(4 + f, LAYERS, stride=8), :] = in_modes
    rows = []
    for cr in range(4):
        here = [ms[row_of(4 * cr + r)] for r in range(4)]
        rows.append(here[0] + here[1] + here[2] + here[3])
    chunk[pl.ds(3, BANDS, stride=4), :] = jnp.broadcast_to(block_mean(rows)[:1], (BANDS, ZONAL))


def coarse_tools(value, masks, fold):
    sub = iota((8, ZONAL), 0)
    lane = iota((8, ZONAL), 1)
    seg = lane % 4
    coriolis = []
    for cr in range(4):
        position = ((seg * 8 + sub) * 4 + cr).astype(F32)
        coriolis.append((4.0 * 0.3) * ((position + 0.5) / float(EXTENT // 4) - 0.5))
    keep = 1.0 - 4.0 * FRICTION
    k = fold[0, 0] // 4
    fold_index = 4 * ((k - lane // 4 + 32) % 32) + 3
    last, top = sub == 7, jnp.logical_and(sub == 7, seg == 3)
    first, bottom = sub == 0, jnp.logical_and(sub == 0, seg == 0)

    def east(x):
        return pltpu.roll(x, ZONAL - 4, 1) - pltpu.roll(x, 4, 1)

    def north(x, sign):
        up = pltpu.roll(x[0], 7, 0)
        up = jnp.where(last, pltpu.roll(up, ZONAL - 1, 1), up)
        up = jnp.where(top, sign * jnp.take_along_axis(x[3], fold_index, axis=1), up)
        down = pltpu.roll(x[3], 1, 0)
        down = jnp.where(first, pltpu.roll(down, 1, 1), down)
        down = jnp.where(bottom, 0.0, down)
        return [x[1] - down, x[2] - x[0], x[3] - x[1], up - x[2]]

    def propagate(state):
        h, u, v = state
        for _ in range(2):
            p = [(0.5 * value) * x for x in h]
            north_p = north(p, 1.0)
            u = [masks[i] * (keep * u[i] + coriolis[i] * v[i] - east(p[i])) for i in range(4)]
            v = [masks[i] * (keep * v[i] - coriolis[i] * u[i] - north_p[i]) for i in range(4)]
            north_v = north(v, -1.0)
            h = [masks[i] * (h[i] - 0.5 * (east(u[i]) + north_v[i])) for i in range(4)]
        return [h, u, v]

    return propagate


def load_state(ref, begin=0):
    return [[ref[begin + f * 32 + cr * 8 : begin + f * 32 + cr * 8 + 8, :] for cr in range(4)] for f in range(3)]


def store_state(ref, state, begin=0):
    for f in range(3):
        for cr in range(4):
            ref[begin + f * 32 + cr * 8 : begin + f * 32 + cr * 8 + 8, :] = state[f][cr]


def add_state(a, b):
    return [[x + y for x, y in zip(p, q)] for p, q in zip(a, b)]


def load_masks(ref):
    return [ref[cr * 8 : cr * 8 + 8, :] for cr in range(4)]


PARTS = 7


def collect_kernel(spread, out):
    for part in range(PARTS):
        at = core_index() * 64 + part + (1 if part > 3 else 0) * 28
        out[part * 8 : part * 8 + 8, :] = spread[pl.ds(at, 8, stride=4), :]


def pair_kernel(half, other_half, values, fold, jumps, mask_out, total):
    seg = iota((8, ZONAL), 1) % 4
    zh = lax.axis_index("zh")
    quarters = [(half, 0, zh), (half, PARTS * 8, zh ^ 1), (other_half, 0, zh ^ 3), (other_half, PARTS * 8, zh ^ 2)]
    for part in range(PARTS):
        rows = [None] * 4
        for ref, begin, quarter in quarters:
            piece = ref[begin + part * 8 : begin + part * 8 + 8, :]
            for cr in range(4):
                moved = pltpu.roll(piece, lax.rem(quarter - cr + ZONAL, ZONAL), 1)
                rows[cr] = moved if rows[cr] is None else jnp.where(seg == quarter, moved, rows[cr])
        for cr in range(4):
            if part == 3:
                mask_out[cr * 8 : cr * 8 + 8, :] = rows[cr]
            else:
                begin = (part if part < 3 else part - 1) * 32 + cr * 8
                jumps[begin : begin + 8, :] = rows[cr]
    propagate = coarse_tools(values[pl.ds(mode_index(), 1), :], load_masks(mask_out), fold)
    store_state(total, add_state(propagate(load_state(jumps)), load_state(jumps, 96)))


def group_kernel(total, mate, mask, values, fold, both):
    propagate = coarse_tools(values[pl.ds(mode_index(), 1), :], load_masks(mask), fold)
    odd = core_index() == 1
    mine, theirs = load_state(total), load_state(mate)
    earlier = [[jnp.where(odd, t, m) for m, t in zip(a, b)] for a, b in zip(mine, theirs)]
    later = [[jnp.where(odd, m, t) for m, t in zip(a, b)] for a, b in zip(mine, theirs)]
    store_state(both, add_state(propagate(propagate(earlier)), later))


def earlier_kernel(two, three, mask, values, fold, out):
    propagate = coarse_tools(values[pl.ds(mode_index(), 1), :], load_masks(mask), fold)
    state = lax.fori_loop(0, 2, lambda _, s: propagate(propagate(s)), load_state(three))
    store_state(out, add_state(state, load_state(two)))


def chain_kernel(one, earlier, mate, jumps, mask, values, fold, chunk):
    quarter = lax.axis_index("zh")
    core = core_index()
    propagate = coarse_tools(values[pl.ds(mode_index(), 1), :], load_masks(mask), fold)

    def twice(state):
        return propagate(propagate(state))

    state = lax.fori_loop(0, 2, lambda _, s: twice(s), load_state(earlier))
    state = add_state(state, load_state(one))
    state = lax.fori_loop(0, core, lambda _, s: add_state(twice(s), load_state(mate)), state)
    seg = iota((8, ZONAL), 1) % 4
    chunk[...] = jnp.zeros_like(chunk)
    for x in range(2):
        state = propagate(state)
        for f in range(3):
            packed = None
            for cr in range(4):
                piece = pltpu.roll(state[f][cr], lax.rem(cr - quarter + ZONAL, ZONAL), 1)
                packed = piece if cr == 0 else jnp.where(seg == cr, piece, packed)
            chunk[pl.ds((2 * core + x) * 32 + f, 8, stride=4), :] = packed
        if x == 0:
            state = add_state(state, load_state(jumps))


def correct_kernel(fine, gathered, vectors, depths, out, result, sems):
    half = lax.axis_index("x") // 2
    lanes = jnp.broadcast_to(depths[...], (LAYERS, LAYERS))
    eye = iota((LAYERS, LAYERS), 0) == iota((LAYERS, LAYERS), 1)
    root = jnp.sqrt(jnp.sum(jnp.where(eye, lanes, 0.0), axis=1, keepdims=True))
    lane = iota((LAYERS, ZONAL), 1)
    copies = []
    for f in range(3):
        in_modes = gathered[pl.ds(half * 4 + f, LAYERS, stride=8), :]
        change = lax.dot_general(
            vectors[:, :LAYERS], in_modes, (((0,), (0,)), ((), ())),
            precision=HIGHEST, preferred_element_type=F32,
        )
        change = change * root if f == 0 else change / root
        for cr in range(4):
            spread = jnp.take_along_axis(change, lane // 4 * 4 + cr, axis=1)
            for r in range(4):
                row = 4 * cr + r
                result[pl.ds(f * 256 + row, LAYERS, stride=BAND), :] = fine[f * BAND + row] + spread
        here = pl.ds(f * 256, 256)
        copies.append(pltpu.make_async_copy(result.at[here], out.at[here], sems.at[f]))
        copies[-1].start()
    for copy in copies:
        copy.wait()


def call(kernel, out_shapes, scratch=(), spaces=None, out_space=pltpu.VMEM, flops=1 << 20, vmem=24 << 20):
    def run(*arrays):
        specs = [pl.BlockSpec(memory_space=s) for s in spaces or (pltpu.VMEM,) * len(arrays)]
        return pl.pallas_call(
            kernel,
            out_shape=[jax.ShapeDtypeStruct(s, F32) for s in out_shapes],
            in_specs=specs,
            out_specs=[pl.BlockSpec(memory_space=out_space)] * len(out_shapes),
            scratch_shapes=list(scratch),
            compiler_params=pltpu.CompilerParams(vmem_limit_bytes=vmem),
            cost_estimate=pl.CostEstimate(flops=flops, bytes_accessed=1 << 20, transcendentals=0),
        )(*arrays)

    return run


def swap(block, axes):
    return lax.all_to_all(block, axes, 0, 0, tiled=True)


def body(start_state, land_mask, fold_map, coupling, depths):
    sent, first, rest, restricted = call(
        pack_kernel,
        [(MASK_AT + BAND, ZONAL), (CUT, ZONAL), (MASK + BAND - CUT, ZONAL), (3 * LAYERS, ZONAL)],
        [pltpu.VMEM((BAND, ZONAL), jnp.int32), pltpu.SemaphoreType.DMA((3,))],
        spaces=(pl.ANY, pl.ANY),
    )(start_state.reshape(MASK, ZONAL), land_mask)
    fold = fold_map.reshape(1, ZONAL)
    depth_row = depths.reshape(1, LAYERS)
    across = [(i, i + 1) for i in range(1, BANDS - 1, 2)]
    across += [(b, a) for a, b in across]
    other = lax.ppermute(sent, SPACE, across)
    following = lax.ppermute(restricted, TIME, [(n + 1, n) for n in range(15)])
    vectors, values = call(modes_kernel, [(LAYERS, ZONAL), (LAYERS, ZONAL)], flops=10 << 20)(
        coupling, depth_row
    )
    inside = [(i, i ^ 1) for i in range(BANDS)]
    mate = [lax.ppermute(part, SPACE, inside) for part in (first, rest)]

    state = pltpu.VMEM((SPAN, 2, 8, ZONAL), F32)
    table = pltpu.VMEM((SPAN, 8, ZONAL), F32)
    scratch = [state, state, state, state, table, table]
    *inner, fold_held = call(
        inner_kernel, [(KEPT, 2, 8, ZONAL)] * 3 + [(1, ZONAL)], scratch, flops=4 << 20
    )(first, rest, *mate, fold, coupling, depth_row)
    fine, chunk = call(
        outer_kernel, [(3 * BAND, LAYERS, ZONAL), (4 * BANDS, ZONAL)], scratch
    )(
        first, rest, other, *inner, fold_held, coupling, depth_row, vectors, following
    )

    spread = swap(chunk, PLANE)
    (mine,) = call(collect_kernel, [(PARTS * 8, ZONAL)])(spread)
    beside = lax.ppermute(mine, ("zh",), [(i, i ^ 1) for i in range(4)])
    half = jnp.concatenate([mine, beside], axis=0)
    other_half = lax.ppermute(half, ("zh",), [(i, i ^ 3) for i in range(4)])
    jumps, mask, total = call(
        pair_kernel, [(192, ZONAL), (32, ZONAL), (96, ZONAL)]
    )(half, other_half, values, fold)
    mate = lax.ppermute(total, ("c",), [(0, 1), (1, 0)])
    (both,) = call(group_kernel, [(96, ZONAL)])(total, mate, mask, values, fold)
    three, two, one = (
        lax.ppermute(both, ("zl",), [(i, i + d) for i in range(4 - d)]) for d in (3, 2, 1)
    )
    (earlier,) = call(earlier_kernel, [(96, ZONAL)])(two, three, mask, values, fold)
    (chunk,) = call(chain_kernel, [(4 * BANDS, ZONAL)])(
        one, earlier, mate, jumps, mask, values, fold
    )
    change = swap(chunk, PLANE)
    (result,) = call(
        correct_kernel,
        [(MASK, ZONAL)],
        [pltpu.VMEM((MASK, ZONAL), F32), pltpu.SemaphoreType.DMA((3,))],
        out_space=pl.ANY,
    )(
        fine, change, vectors, depth_row
    )
    return result.reshape(1, 3, LAYERS, BAND, ZONAL)


def solution(mesh):
    parts = Mesh(mesh.devices.reshape(4, 4, 4, 4, 2), ("zl", "x", "zh", "y", "c"))
    return jax.shard_map(
        body,
        mesh=parts,
        in_specs=(P(TIME, None, None, SPACE, None), P(SPACE, None), P(), P(), P()),
        out_specs=P(TIME, None, None, SPACE, None),
        check_vma=False,
    )
```

```python
import functools

import jax
import jax.numpy as jnp
from jax import lax
from jax.experimental import pallas as pl
from jax.experimental.pallas import tpu as pltpu
from jax.sharding import Mesh
from jax.sharding import PartitionSpec as P

LAYERS = 16
ZONAL = 128
FINE_STEPS = 8
BAND = 16
BANDS = 32
EXTENT = BAND * BANDS
HALO = 2 * FINE_STEPS
SPAN = BAND + 2 * HALO
FRICTION = 0.02
CUT = 2 * LAYERS * BAND
MASK = 3 * LAYERS * BAND
HIGHEST = lax.Precision.HIGHEST
F32 = jnp.float32
BF16 = jnp.bfloat16

SPACE = ("zh", "y", "c")
TIME = ("zl", "x")
PLANE = ("x", "y", "c")

SHIFT = 1.0


def iota(shape, axis):
    return lax.broadcasted_iota(jnp.int32, shape, axis)


def two_parts(x):
    top = x.astype(BF16)
    return top, (x - top.astype(F32)).astype(BF16)


def dot3(a, b):
    (a_top, a_rest), (b_top, b_rest) = two_parts(a), two_parts(b)
    left = jnp.concatenate([a_top, a_top, a_rest], axis=1)
    right = jnp.concatenate([b_top, b_rest, b_top], axis=0)
    return jnp.dot(left, right, preferred_element_type=F32)


def block_mean(rows):
    part = iota(rows[0].shape, 1) % 4

    def pairs(x, y, step):
        first = (part & step) == 0
        return jnp.where(first, x + pltpu.roll(x, ZONAL - step, 1), y + pltpu.roll(y, step, 1))

    return pairs(pairs(rows[0], rows[1], 1), pairs(rows[2], rows[3], 1), 2) * (1.0 / 16.0)


VELOCITY_AT = (0, LAYERS * BAND, LAYERS * (2 * BAND - 1))
MASK_AT = LAYERS * (3 * BAND - 2)


def pack_kernel(state, mask, sent, first, rest, restricted, sems):
    copies = [
        pltpu.make_async_copy(state.at[pl.ds(0, CUT)], first, sems.at[0]),
        pltpu.make_async_copy(state.at[pl.ds(CUT, MASK - CUT)], rest.at[pl.ds(0, MASK - CUT)], sems.at[1]),
        pltpu.make_async_copy(mask, rest.at[pl.ds(MASK - CUT, BAND)], sems.at[2]),
    ]
    for copy in copies:
        copy.start()
    for copy in copies:
        copy.wait()

    def row_of(f, r):
        if f < 2:
            return first[pl.ds(f * 256 + r, LAYERS, stride=BAND), :]
        return rest[pl.ds(r, LAYERS, stride=BAND), :]

    for odd in (False, True):

        @pl.when(core_index() == int(odd))
        def _():
            for k in range(BAND):
                r = BAND - 1 - k if odd else k
                for f in range(3 if k < BAND - 1 else 1):
                    at = VELOCITY_AT[f] + LAYERS * k
                    sent[at : at + LAYERS, :] = row_of(f, r)
                sent[MASK_AT + k : MASK_AT + k + 1, :] = rest[MASK - CUT + r : MASK - CUT + r + 1, :]

    for f in range(3):
        rows = []
        for cr in range(4):
            here = [row_of(f, 4 * cr + r) for r in range(4)]
            rows.append(here[0] + here[1] + here[2] + here[3])
        restricted[f * LAYERS : (f + 1) * LAYERS, :] = block_mean(rows)


def modes_kernel(coupling, depths, vectors, values):
    row = iota((LAYERS, ZONAL), 0)
    lane = iota((LAYERS, ZONAL), 1)
    eye = row == lane
    root = jnp.sqrt(depths[...])
    root = jnp.concatenate([root, jnp.zeros((1, ZONAL - LAYERS), F32)], axis=1)
    root_lanes = jnp.broadcast_to(root, (LAYERS, ZONAL))
    root_rows = jnp.sum(jnp.where(eye, root_lanes, 0.0), axis=1, keepdims=True)
    matrix = jnp.concatenate([coupling[...], jnp.zeros((LAYERS, ZONAL - LAYERS), F32)], axis=1)
    matrix = matrix * root_lanes * root_rows
    start = matrix + jnp.where(eye, SHIFT, 0.0) + jnp.where(lane == row + LAYERS, 1.0, 0.0)
    active = iota((8, ZONAL), 1) < LAYERS
    sub = iota((8, ZONAL), 0)

    def sums(x):
        return jnp.broadcast_to(jnp.sum(jnp.where(active, x, 0.0), axis=1, keepdims=True), x.shape)

    def turn(width, x):
        if width == 8:
            return pltpu.roll(x, 1, 0)
        return jnp.where((sub & (width - 1)) == 0, pltpu.roll(x, 9 - width, 0), pltpu.roll(x, 1, 0))

    def regroup(half, x, y):
        low = (sub & half) == 0
        return jnp.where(low, x, pltpu.roll(y, half, 0)), jnp.where(low, pltpu.roll(x, 8 - half, 0), y)

    def sweep(carry):
        count, _, x, y = carry
        xx, yy = sums(x * x), sums(y * y)
        worst = jnp.zeros((8, ZONAL), F32)
        for width in (8, 4, 2, 1):
            for _ in range(width):
                xy = sums(x * y)
                gap = yy - xx
                side = jnp.maximum(jnp.abs(gap), 1e-12)
                scale = lax.rsqrt(side * side + 4.0 * xy * xy)
                square = 0.5 + 0.5 * side * scale
                cosine_over = lax.rsqrt(square)
                signed = jnp.where(gap >= 0.0, xy, -xy) * scale
                cosine = square * cosine_over
                sine = signed * cosine_over
                tangent_xy = signed * xy / square
                worst = jnp.maximum(worst, jnp.abs(xy))
                x, y = cosine * x - sine * y, sine * x + cosine * y
                xx, yy = xx - tangent_xy, yy + tangent_xy
                if width > 1:
                    y, yy = turn(width, y), turn(width, yy)
            if width > 1:
                x, y = regroup(width // 2, x, y)
                xx, yy = regroup(width // 2, xx, yy)
        return count + 1, jnp.max(worst), x, y

    def unfinished(carry):
        return jnp.logical_and(carry[0] < 12, carry[1] > 2e-4)

    _, _, x, y = lax.while_loop(unfinished, sweep, (0, jnp.float32(1.0), start[:8], start[8:]))
    x = jnp.concatenate([x, y], axis=0)
    active = lane < LAYERS
    turned = pltpu.roll(x, ZONAL - LAYERS, 1)
    vectors[...] = jnp.where(active, turned, 0.0)
    value = jnp.sum(jnp.where(active, x * turned, 0.0), axis=1, keepdims=True) - SHIFT
    values[...] = jnp.broadcast_to(value, (LAYERS, ZONAL))


def east(x):
    flat = x.reshape(-1, ZONAL)
    return (pltpu.roll(flat, ZONAL - 1, 1) - pltpu.roll(flat, 1, 1)).reshape(x.shape)


def fine_tools(fields, ps, ms, fs, coupling, depths):
    hs, us, vs = fields
    half_top, half_rest = two_parts(0.5 * coupling[...])
    weights = jnp.concatenate([half_top, half_top, half_rest], axis=1)
    lanes = jnp.broadcast_to(depths[...], (LAYERS, LAYERS))
    eye = iota((LAYERS, LAYERS), 0) == iota((LAYERS, LAYERS), 1)
    thick = 0.5 * jnp.sum(jnp.where(eye, lanes, 0.0), axis=1, keepdims=True)
    thick = jnp.broadcast_to(thick, (LAYERS, ZONAL)).reshape(1, 2, 8, ZONAL)
    keep = 1.0 - FRICTION

    def pressure(low, high):
        wide = jnp.concatenate([hs[j].reshape(LAYERS, ZONAL) for j in range(low, high)], axis=1)
        top, rest = two_parts(wide)
        stacked = jnp.concatenate([top, rest, top], axis=0)
        result = jnp.dot(weights, stacked, preferred_element_type=F32)
        for j in range(low, high):
            ps[j] = result[:, (j - low) * ZONAL : (j - low + 1) * ZONAL].reshape(2, 8, ZONAL)

    def velocity(low, high):
        m = ms[low:high][:, None]
        f = fs[low:high][:, None]
        u = us[low:high]
        v = vs[low:high]
        u = m * (keep * u + f * v - east(ps[low:high]))
        v = m * (keep * v - f * u - (ps[low + 1 : high + 1] - ps[low - 1 : high - 1]))
        us[low:high] = u
        vs[low:high] = v

    def thickness(low, high):
        m = ms[low:high][:, None]
        spread = east(us[low:high]) + (vs[low + 1 : high + 1] - vs[low - 1 : high - 1])
        hs[low:high] = m * (hs[low:high] - thick * spread)

    def steps(bounds):
        for low, ends in bounds:
            for at in range(low, ends[0], 4):
                pressure(at, min(at + 4, ends[0]))
            for at in range(low + 1, ends[1], 4):
                velocity(at, min(at + 4, ends[1]))
            for at in range(low + 2, ends[2], 4):
                thickness(at, min(at + 4, ends[2]))

    return steps


def core_index():
    return lax.axis_index("c")


def band_index():
    return lax.axis_index("zh") * 8 + lax.axis_index("y") * 2 + lax.axis_index("c")


def mode_index():
    return lax.axis_index("x") * 4 + lax.axis_index("y")


def put_band(fields, ms, begin, blocks, core, sign):
    for odd in (False, True):

        @pl.when(core == int(odd))
        def _():
            for r in range(BAND):
                row = begin + (BAND - 1 - r if odd else r)
                for f in range(3):
                    at = f * 256 + r - (CUT if f == 2 else 0)
                    value = blocks[f // 2][pl.ds(at, LAYERS, stride=BAND), :].reshape(2, 8, ZONAL)
                    fields[f][row] = sign * value if f == 2 else value
                at = MASK - CUT + r
                ms[row] = jnp.broadcast_to(blocks[1][at : at + 1, :], (8, ZONAL))


def coriolis_table(fs, position, core, sign):
    offset = iota(fs.shape, 0) - HALO
    rows = position * BAND + jnp.where(core == 1, BAND - 1 - offset, offset)
    latitude = (rows.astype(F32) + 0.5) / float(EXTENT)
    latitude = jnp.where(latitude > 1.0, 2.0 - latitude, latitude)
    fs[...] = sign * (0.3 * (latitude - 0.5))


KEPT = 20


def inner_kernel(
    own_first, own_rest, mate_first, mate_rest, fold, coupling, depths, h_out, u_out, v_out, fold_out, hs, us, vs, ps, ms, fs
):
    core = core_index()
    sign = (1 - 2 * core).astype(F32)
    fields = (hs, us, vs)
    put_band(fields, ms, HALO, (own_first, own_rest), core, sign)
    put_band(fields, ms, HALO + BAND, (mate_first, mate_rest), core, sign)
    coriolis_table(fs, band_index(), core, sign)
    steps = fine_tools(fields, ps, ms, fs, coupling, depths)
    ends = [SPAN - 2 * t for t in range(FINE_STEPS)]
    steps([(HALO + 2 * t, (ends[t], ends[t] - 1, ends[t] - 2)) for t in range(FINE_STEPS)])
    fold_out[...] = fold[...].astype(F32)
    for out, field in zip((h_out, u_out, v_out), fields):
        out[...] = field[HALO : HALO + KEPT]


def outer_kernel(
    own_first, own_rest, other, h_in, u_in, v_in, fold, coupling, depths, vectors, following,
    fine, chunk, hs, us, vs, ps, ms, fs,
):
    position = band_index()
    core = core_index()
    sign = (1 - 2 * core).astype(F32)
    on_top = position == BANDS - 1
    fields = (hs, us, vs)
    for field, kept in zip(fields, (h_in, u_in, v_in)):
        field[HALO : HALO + KEPT] = kept[...]
    for r in range(BAND):
        row = HALO + r + core * (BAND - 1 - 2 * r)
        ms[row] = jnp.broadcast_to(own_rest[MASK - CUT + r : MASK - CUT + r + 1, :], (8, ZONAL))

    @pl.when(jnp.logical_not(on_top))
    def _():
        for k in range(BAND):
            for f in range(3 if k < BAND - 1 else 1):
                at = VELOCITY_AT[f] + LAYERS * k
                value = other[at : at + LAYERS, :].reshape(2, 8, ZONAL)
                fields[f][BAND - 1 - k] = sign * value if f == 2 else value
            ms[BAND - 1 - k] = jnp.broadcast_to(other[MASK_AT + k : MASK_AT + k + 1, :], (8, ZONAL))

    @pl.when(on_top)
    def _():
        index = jnp.broadcast_to(fold[...].astype(jnp.int32), (LAYERS, ZONAL))
        for r in range(BAND):
            for f in range(3):
                block, at = (own_first, f * 256 + r) if f < 2 else (own_rest, r)
                image = block[pl.ds(at, LAYERS, stride=BAND), :]
                image = jnp.take_along_axis(image, index, axis=1).reshape(2, 8, ZONAL)
                fields[f][r] = -image if f == 1 else image
            image = jnp.broadcast_to(own_rest[MASK - CUT + r : MASK - CUT + r + 1, :], (8, ZONAL))
            ms[r] = jnp.take_along_axis(image, index[:8], axis=1)

    coriolis_table(fs, position, core, sign)
    steps = fine_tools(fields, ps, ms, fs, coupling, depths)
    steps([(2 * t, (2 * t + 18, 2 * t + 17, 2 * t + 18)) for t in range(FINE_STEPS)])

    def row_of(r):
        return HALO + r + core * (BAND - 1 - 2 * r)

    root = jnp.sqrt(depths[...])
    jumps = []
    for f in range(3):
        rows = []
        for cr in range(4):
            here = [fields[f][row_of(4 * cr + r)].reshape(LAYERS, ZONAL) for r in range(4)]
            if f == 2:
                here = [sign * row for row in here]
            for r in range(4):
                fine[f * BAND + 4 * cr + r] = here[r]
            rows.append(here[0] + here[1] + here[2] + here[3])
        jumps.append(block_mean(rows) - following[f * LAYERS : (f + 1) * LAYERS, :])
    of_thickness = dot3(vectors[:, :LAYERS] / root, jumps[0])
    of_velocity = dot3(vectors[:, :LAYERS] * root, jnp.concatenate(jumps[1:], axis=1))
    for f, in_modes in enumerate((of_thickness, of_velocity[:, :ZONAL], of_velocity[:, ZONAL:])):
        chunk[pl.ds(f, LAYERS, stride=8), :] = in_modes
        chunk[pl.ds(4 + f, LAYERS, stride=8), :] = in_modes
    rows = []
    for cr in range(4):
        here = [ms[row_of(4 * cr + r)] for r in range(4)]
        rows.append(here[0] + here[1] + here[2] + here[3])
    chunk[pl.ds(3, BANDS, stride=4), :] = jnp.broadcast_to(block_mean(rows)[:1], (BANDS, ZONAL))


def coarse_tools(value, masks, fold):
    sub = iota((8, ZONAL), 0)
    lane = iota((8, ZONAL), 1)
    seg = lane % 4
    coriolis = []
    for cr in range(4):
        position = ((seg * 8 + sub) * 4 + cr).astype(F32)
        coriolis.append((4.0 * 0.3) * ((position + 0.5) / float(EXTENT // 4) - 0.5))
    keep = 1.0 - 4.0 * FRICTION
    k = fold[0, 0] // 4
    fold_index = 4 * ((k - lane // 4 + 32) % 32) + 3
    last, top = sub == 7, jnp.logical_and(sub == 7, seg == 3)
    first, bottom = sub == 0, jnp.logical_and(sub == 0, seg == 0)

    def east(x):
        return pltpu.roll(x, ZONAL - 4, 1) - pltpu.roll(x, 4, 1)

    def north(x, sign):
        up = pltpu.roll(x[0], 7, 0)
        up = jnp.where(last, pltpu.roll(up, ZONAL - 1, 1), up)
        up = jnp.where(top, sign * jnp.take_along_axis(x[3], fold_index, axis=1), up)
        down = pltpu.roll(x[3], 1, 0)
        down = jnp.where(first, pltpu.roll(down, 1, 1), down)
        down = jnp.where(bottom, 0.0, down)
        return [x[1] - down, x[2] - x[0], x[3] - x[1], up - x[2]]

    kept = [keep * m for m in masks]
    turned = [m * f for m, f in zip(masks, coriolis)]
    pushed = [(0.5 * value) * m for m in masks]
    spread = [0.5 * m for m in masks]

    def propagate(state):
        h, u, v = state
        for _ in range(2):
            north_h = north(h, 1.0)
            slow = [kept[i] * v[i] - pushed[i] * north_h[i] for i in range(4)]
            u = [(kept[i] * u[i] + turned[i] * v[i]) - pushed[i] * east(h[i]) for i in range(4)]
            v = [slow[i] - turned[i] * u[i] for i in range(4)]
            rest = [masks[i] * h[i] - spread[i] * east(u[i]) for i in range(4)]
            north_v = north(v, -1.0)
            h = [rest[i] - spread[i] * north_v[i] for i in range(4)]
        return [h, u, v]

    return propagate


def load_state(ref, begin=0):
    return [[ref[begin + f * 32 + cr * 8 : begin + f * 32 + cr * 8 + 8, :] for cr in range(4)] for f in range(3)]


def store_state(ref, state, begin=0):
    for f in range(3):
        for cr in range(4):
            ref[begin + f * 32 + cr * 8 : begin + f * 32 + cr * 8 + 8, :] = state[f][cr]


def add_state(a, b):
    return [[x + y for x, y in zip(p, q)] for p, q in zip(a, b)]


def load_masks(ref):
    return [ref[cr * 8 : cr * 8 + 8, :] for cr in range(4)]


PARTS = 7


def collect_kernel(spread, out):
    for part in range(PARTS):
        at = core_index() * 64 + part + (1 if part > 3 else 0) * 28
        out[part * 8 : part * 8 + 8, :] = spread[pl.ds(at, 8, stride=4), :]


def pair_kernel(half, other_half, values, fold, jumps, mask_out, total):
    seg = iota((8, ZONAL), 1) % 4
    zh = lax.axis_index("zh")
    quarters = [(half, 0, zh), (half, PARTS * 8, zh ^ 1), (other_half, 0, zh ^ 3), (other_half, PARTS * 8, zh ^ 2)]
    for part in range(PARTS):
        rows = [None] * 4
        for ref, begin, quarter in quarters:
            piece = ref[begin + part * 8 : begin + part * 8 + 8, :]
            for cr in range(4):
                moved = pltpu.roll(piece, lax.rem(quarter - cr + ZONAL, ZONAL), 1)
                rows[cr] = moved if rows[cr] is None else jnp.where(seg == quarter, moved, rows[cr])
        for cr in range(4):
            if part == 3:
                mask_out[cr * 8 : cr * 8 + 8, :] = rows[cr]
            else:
                begin = (part if part < 3 else part - 1) * 32 + cr * 8
                jumps[begin : begin + 8, :] = rows[cr]
    propagate = coarse_tools(values[pl.ds(mode_index(), 1), :], load_masks(mask_out), fold)
    store_state(total, add_state(propagate(load_state(jumps)), load_state(jumps, 96)))


def group_kernel(total, mate, mask, values, fold, both):
    propagate = coarse_tools(values[pl.ds(mode_index(), 1), :], load_masks(mask), fold)
    odd = core_index() == 1
    mine, theirs = load_state(total), load_state(mate)
    earlier = [[jnp.where(odd, t, m) for m, t in zip(a, b)] for a, b in zip(mine, theirs)]
    later = [[jnp.where(odd, m, t) for m, t in zip(a, b)] for a, b in zip(mine, theirs)]
    trips = jnp.where(lax.axis_index("zl") < 3, 1, 0)
    state = lax.fori_loop(0, trips, lambda _, s: propagate(propagate(s)), earlier)
    store_state(both, add_state(state, later))


def repeat(wanted, propagate, state):
    return lax.fori_loop(0, jnp.where(wanted, 2, 0), lambda _, s: propagate(propagate(s)), state)


def earlier_kernel(three, mask, values, fold, out):
    propagate = coarse_tools(values[pl.ds(mode_index(), 1), :], load_masks(mask), fold)
    store_state(out, repeat(lax.axis_index("zl") == 3, propagate, load_state(three)))


def chain_kernel(one, two, earlier, mate, jumps, mask, values, fold, chunk):
    quarter = lax.axis_index("zh")
    core = core_index()
    propagate = coarse_tools(values[pl.ds(mode_index(), 1), :], load_masks(mask), fold)

    def twice(state):
        return propagate(propagate(state))

    state = add_state(load_state(earlier), load_state(two))
    state = repeat(lax.axis_index("zl") >= 2, propagate, state)
    state = add_state(state, load_state(one))
    state = lax.fori_loop(0, core, lambda _, s: add_state(twice(s), load_state(mate)), state)
    seg = iota((8, ZONAL), 1) % 4
    chunk[...] = jnp.zeros_like(chunk)
    for x in range(2):
        state = propagate(state)
        for f in range(3):
            packed = None
            for cr in range(4):
                piece = pltpu.roll(state[f][cr], lax.rem(cr - quarter + ZONAL, ZONAL), 1)
                packed = piece if cr == 0 else jnp.where(seg == cr, piece, packed)
            chunk[pl.ds((2 * core + x) * 32 + f, 8, stride=4), :] = packed
        if x == 0:
            state = add_state(state, load_state(jumps))


def correct_kernel(fine, gathered, vectors, depths, out, result, sems):
    half = lax.axis_index("x") // 2
    lanes = jnp.broadcast_to(depths[...], (LAYERS, LAYERS))
    eye = iota((LAYERS, LAYERS), 0) == iota((LAYERS, LAYERS), 1)
    root = jnp.sqrt(jnp.sum(jnp.where(eye, lanes, 0.0), axis=1, keepdims=True))
    lane = iota((LAYERS, ZONAL), 1)
    copies = []
    for f in range(3):
        in_modes = gathered[pl.ds(half * 4 + f, LAYERS, stride=8), :]
        change = lax.dot_general(
            vectors[:, :LAYERS], in_modes, (((0,), (0,)), ((), ())),
            precision=HIGHEST, preferred_element_type=F32,
        )
        change = change * root if f == 0 else change / root
        for cr in range(4):
            spread = jnp.take_along_axis(change, lane // 4 * 4 + cr, axis=1)
            for r in range(4):
                row = 4 * cr + r
                result[pl.ds(f * 256 + row, LAYERS, stride=BAND), :] = fine[f * BAND + row] + spread
        here = pl.ds(f * 256, 256)
        copies.append(pltpu.make_async_copy(result.at[here], out.at[here], sems.at[f]))
        copies[-1].start()
    for copy in copies:
        copy.wait()


def call(kernel, out_shapes, scratch=(), spaces=None, out_space=pltpu.VMEM, flops=1 << 20, vmem=24 << 20):
    def run(*arrays):
        specs = [pl.BlockSpec(memory_space=s) for s in spaces or (pltpu.VMEM,) * len(arrays)]
        return pl.pallas_call(
            kernel,
            out_shape=[jax.ShapeDtypeStruct(s, F32) for s in out_shapes],
            in_specs=specs,
            out_specs=[pl.BlockSpec(memory_space=out_space)] * len(out_shapes),
            scratch_shapes=list(scratch),
            compiler_params=pltpu.CompilerParams(vmem_limit_bytes=vmem),
            cost_estimate=pl.CostEstimate(flops=flops, bytes_accessed=1 << 20, transcendentals=0),
        )(*arrays)

    return run


def swap(block, axes):
    return lax.all_to_all(block, axes, 0, 0, tiled=True)


def body(start_state, land_mask, fold_map, coupling, depths):
    sent, first, rest, restricted = call(
        pack_kernel,
        [(MASK_AT + BAND, ZONAL), (CUT, ZONAL), (MASK + BAND - CUT, ZONAL), (3 * LAYERS, ZONAL)],
        [pltpu.SemaphoreType.DMA((3,))],
        spaces=(pl.ANY, pl.ANY),
    )(start_state.reshape(MASK, ZONAL), land_mask.astype(F32))
    fold = fold_map.reshape(1, ZONAL)
    depth_row = depths.reshape(1, LAYERS)
    across = [(i, i + 1) for i in range(1, BANDS - 1, 2)]
    across += [(b, a) for a, b in across]
    other = lax.ppermute(sent, SPACE, across)
    following = lax.ppermute(restricted, TIME, [(n + 1, n) for n in range(15)])
    vectors, values = call(modes_kernel, [(LAYERS, ZONAL), (LAYERS, ZONAL)], flops=10 << 20)(
        coupling, depth_row
    )
    inside = [(i, i ^ 1) for i in range(BANDS)]
    mate = [lax.ppermute(part, SPACE, inside) for part in (first, rest)]

    state = pltpu.VMEM((SPAN, 2, 8, ZONAL), F32)
    table = pltpu.VMEM((SPAN, 8, ZONAL), F32)
    scratch = [state, state, state, state, table, table]
    *inner, fold_held = call(
        inner_kernel, [(KEPT, 2, 8, ZONAL)] * 3 + [(1, ZONAL)], scratch, flops=4 << 20
    )(first, rest, *mate, fold, coupling, depth_row)
    fine, chunk = call(
        outer_kernel, [(3 * BAND, LAYERS, ZONAL), (4 * BANDS, ZONAL)], scratch
    )(
        first, rest, other, *inner, fold_held, coupling, depth_row, vectors, following
    )

    spread = swap(chunk, PLANE)
    (mine,) = call(collect_kernel, [(PARTS * 8, ZONAL)])(spread)
    beside = lax.ppermute(mine, ("zh",), [(i, i ^ 1) for i in range(4)])
    half = jnp.concatenate([mine, beside], axis=0)
    other_half = lax.ppermute(half, ("zh",), [(i, i ^ 3) for i in range(4)])
    jumps, mask, total = call(
        pair_kernel, [(192, ZONAL), (32, ZONAL), (96, ZONAL)]
    )(half, other_half, values, fold)
    mate = lax.ppermute(total, ("c",), [(0, 1), (1, 0)])
    (both,) = call(group_kernel, [(96, ZONAL)])(total, mate, mask, values, fold)
    three, two, one = (
        lax.ppermute(both, ("zl",), [(i, i + d) for i in range(4 - d)]) for d in (3, 2, 1)
    )
    (earlier,) = call(earlier_kernel, [(96, ZONAL)])(three, mask, values, fold)
    (chunk,) = call(chain_kernel, [(4 * BANDS, ZONAL)])(
        one, two, earlier, mate, jumps, mask, values, fold
    )
    change = swap(chunk, PLANE)
    (result,) = call(
        correct_kernel,
        [(MASK, ZONAL)],
        [pltpu.VMEM((MASK, ZONAL), F32), pltpu.SemaphoreType.DMA((3,))],
        out_space=pl.ANY,
    )(
        fine, change, vectors, depth_row
    )
    return result.reshape(1, 3, LAYERS, BAND, ZONAL)


def solution(mesh):
    parts = Mesh(mesh.devices.reshape(4, 4, 4, 4, 2), ("zl", "x", "zh", "y", "c"))
    return jax.shard_map(
        body,
        mesh=parts,
        in_specs=(P(TIME, None, None, SPACE, None), P(SPACE, None), P(), P(), P()),
        out_specs=P(TIME, None, None, SPACE, None),
        check_vma=False,
    )
```

```python
import functools

import jax
import jax.numpy as jnp
from jax import lax
from jax.experimental import pallas as pl
from jax.experimental.pallas import tpu as pltpu
from jax.sharding import Mesh
from jax.sharding import PartitionSpec as P

LAYERS = 16
ZONAL = 128
FINE_STEPS = 8
BAND = 16
BANDS = 32
EXTENT = BAND * BANDS
HALO = 2 * FINE_STEPS
SPAN = BAND + 2 * HALO
FRICTION = 0.02
CUT = 2 * LAYERS * BAND
MASK = 3 * LAYERS * BAND
HIGHEST = lax.Precision.HIGHEST
F32 = jnp.float32
BF16 = jnp.bfloat16

SPACE = ("zh", "y", "c")
TIME = ("zl", "x")
PLANE = ("x", "y", "c")

SHIFT = 1.0


def iota(shape, axis):
    return lax.broadcasted_iota(jnp.int32, shape, axis)


def two_parts(x):
    top = x.astype(BF16)
    return top, (x - top.astype(F32)).astype(BF16)


def dot3(a, b):
    (a_top, a_rest), (b_top, b_rest) = two_parts(a), two_parts(b)
    left = jnp.concatenate([a_top, a_top, a_rest], axis=1)
    right = jnp.concatenate([b_top, b_rest, b_top], axis=0)
    return jnp.dot(left, right, preferred_element_type=F32)


def block_mean(rows):
    part = iota(rows[0].shape, 1) % 4

    def pairs(x, y, step):
        first = (part & step) == 0
        return jnp.where(first, x + pltpu.roll(x, ZONAL - step, 1), y + pltpu.roll(y, step, 1))

    return pairs(pairs(rows[0], rows[1], 1), pairs(rows[2], rows[3], 1), 2) * (1.0 / 16.0)


VELOCITY_AT = (0, LAYERS * BAND, LAYERS * (2 * BAND - 1))
MASK_AT = LAYERS * (3 * BAND - 2)


def pack_kernel(state, mask, sent, first, rest, restricted, sems):
    copies = [
        pltpu.make_async_copy(state.at[pl.ds(0, CUT)], first, sems.at[0]),
        pltpu.make_async_copy(state.at[pl.ds(CUT, MASK - CUT)], rest.at[pl.ds(0, MASK - CUT)], sems.at[1]),
        pltpu.make_async_copy(mask, rest.at[pl.ds(MASK - CUT, BAND)], sems.at[2]),
    ]
    for copy in copies:
        copy.start()
    for copy in copies:
        copy.wait()

    def row_of(f, r):
        if f < 2:
            return first[pl.ds(f * 256 + r, LAYERS, stride=BAND), :]
        return rest[pl.ds(r, LAYERS, stride=BAND), :]

    for odd in (False, True):

        @pl.when(core_index() == int(odd))
        def _():
            for k in range(BAND):
                r = BAND - 1 - k if odd else k
                for f in range(3 if k < BAND - 1 else 1):
                    at = VELOCITY_AT[f] + LAYERS * k
                    sent[at : at + LAYERS, :] = row_of(f, r)
                sent[MASK_AT + k : MASK_AT + k + 1, :] = rest[MASK - CUT + r : MASK - CUT + r + 1, :]

    for f in range(3):
        rows = []
        for cr in range(4):
            here = [row_of(f, 4 * cr + r) for r in range(4)]
            rows.append(here[0] + here[1] + here[2] + here[3])
        restricted[f * LAYERS : (f + 1) * LAYERS, :] = block_mean(rows)


def modes_kernel(coupling, depths, vectors, values):
    row = iota((LAYERS, ZONAL), 0)
    lane = iota((LAYERS, ZONAL), 1)
    eye = row == lane
    root = jnp.sqrt(depths[...])
    root = jnp.concatenate([root, jnp.zeros((1, ZONAL - LAYERS), F32)], axis=1)
    root_lanes = jnp.broadcast_to(root, (LAYERS, ZONAL))
    root_rows = jnp.sum(jnp.where(eye, root_lanes, 0.0), axis=1, keepdims=True)
    matrix = jnp.concatenate([coupling[...], jnp.zeros((LAYERS, ZONAL - LAYERS), F32)], axis=1)
    matrix = matrix * root_lanes * root_rows
    start = matrix + jnp.where(eye, SHIFT, 0.0) + jnp.where(lane == row + LAYERS, 1.0, 0.0)
    active = iota((8, ZONAL), 1) < LAYERS
    sub = iota((8, ZONAL), 0)

    def sums(x):
        return jnp.broadcast_to(jnp.sum(jnp.where(active, x, 0.0), axis=1, keepdims=True), x.shape)

    def turn(width, x):
        if width == 8:
            return pltpu.roll(x, 1, 0)
        return jnp.where((sub & (width - 1)) == 0, pltpu.roll(x, 9 - width, 0), pltpu.roll(x, 1, 0))

    def regroup(half, x, y):
        low = (sub & half) == 0
        return jnp.where(low, x, pltpu.roll(y, half, 0)), jnp.where(low, pltpu.roll(x, 8 - half, 0), y)

    def sweep(carry):
        count, _, x, y = carry
        xx, yy = sums(x * x), sums(y * y)
        worst = jnp.zeros((8, ZONAL), F32)
        for width in (8, 4, 2, 1):
            for _ in range(width):
                xy = sums(x * y)
                gap = yy - xx
                side = jnp.maximum(jnp.abs(gap), 1e-12)
                scale = lax.rsqrt(side * side + 4.0 * xy * xy)
                square = 0.5 + 0.5 * side * scale
                cosine_over = lax.rsqrt(square)
                signed = jnp.where(gap >= 0.0, xy, -xy) * scale
                cosine = square * cosine_over
                sine = signed * cosine_over
                tangent_xy = signed * xy / square
                worst = jnp.maximum(worst, jnp.abs(xy))
                x, y = cosine * x - sine * y, sine * x + cosine * y
                xx, yy = xx - tangent_xy, yy + tangent_xy
                if width > 1:
                    y, yy = turn(width, y), turn(width, yy)
            if width > 1:
                x, y = regroup(width // 2, x, y)
                xx, yy = regroup(width // 2, xx, yy)
        return count + 1, jnp.max(worst), x, y

    def unfinished(carry):
        return jnp.logical_and(carry[0] < 12, carry[1] > 2e-4)

    _, _, x, y = lax.while_loop(unfinished, sweep, (0, jnp.float32(1.0), start[:8], start[8:]))
    x = jnp.concatenate([x, y], axis=0)
    active = lane < LAYERS
    turned = pltpu.roll(x, ZONAL - LAYERS, 1)
    vectors[...] = jnp.where(active, turned, 0.0)
    value = jnp.sum(jnp.where(active, x * turned, 0.0), axis=1, keepdims=True) - SHIFT
    values[...] = jnp.broadcast_to(value, (LAYERS, ZONAL))


def east(x):
    flat = x.reshape(-1, ZONAL)
    return (pltpu.roll(flat, ZONAL - 1, 1) - pltpu.roll(flat, 1, 1)).reshape(x.shape)


def fine_tools(fields, ps, ms, fs, coupling, depths):
    hs, us, vs = fields
    half_top, half_rest = two_parts(0.5 * coupling[...])
    weights = jnp.concatenate([half_top, half_top, half_rest], axis=1)
    lanes = jnp.broadcast_to(depths[...], (LAYERS, LAYERS))
    eye = iota((LAYERS, LAYERS), 0) == iota((LAYERS, LAYERS), 1)
    thick = 0.5 * jnp.sum(jnp.where(eye, lanes, 0.0), axis=1, keepdims=True)
    thick = jnp.broadcast_to(thick, (LAYERS, ZONAL)).reshape(1, 2, 8, ZONAL)
    keep = 1.0 - FRICTION

    def pressure(low, high):
        wide = jnp.concatenate([hs[j].reshape(LAYERS, ZONAL) for j in range(low, high)], axis=1)
        top, rest = two_parts(wide)
        stacked = jnp.concatenate([top, rest, top], axis=0)
        result = jnp.dot(weights, stacked, preferred_element_type=F32)
        for j in range(low, high):
            ps[j] = result[:, (j - low) * ZONAL : (j - low + 1) * ZONAL].reshape(2, 8, ZONAL)

    def velocity(low, high):
        m = ms[low:high][:, None]
        f = fs[low:high][:, None]
        u = us[low:high]
        v = vs[low:high]
        u = m * (keep * u + f * v - east(ps[low:high]))
        v = m * (keep * v - f * u - (ps[low + 1 : high + 1] - ps[low - 1 : high - 1]))
        us[low:high] = u
        vs[low:high] = v

    def thickness(low, high):
        m = ms[low:high][:, None]
        spread = east(us[low:high]) + (vs[low + 1 : high + 1] - vs[low - 1 : high - 1])
        hs[low:high] = m * (hs[low:high] - thick * spread)

    def steps(bounds):
        for low, ends in bounds:
            for at in range(low, ends[0], 4):
                pressure(at, min(at + 4, ends[0]))
            for at in range(low + 1, ends[1], 4):
                velocity(at, min(at + 4, ends[1]))
            for at in range(low + 2, ends[2], 4):
                thickness(at, min(at + 4, ends[2]))

    return steps


def core_index():
    return lax.axis_index("c")


def band_index():
    return lax.axis_index("zh") * 8 + lax.axis_index("y") * 2 + lax.axis_index("c")


def mode_index():
    return lax.axis_index("x") * 4 + lax.axis_index("y")


def put_band(fields, ms, begin, blocks, core, sign):
    for odd in (False, True):

        @pl.when(core == int(odd))
        def _():
            for r in range(BAND):
                row = begin + (BAND - 1 - r if odd else r)
                for f in range(3):
                    at = f * 256 + r - (CUT if f == 2 else 0)
                    value = blocks[f // 2][pl.ds(at, LAYERS, stride=BAND), :].reshape(2, 8, ZONAL)
                    fields[f][row] = sign * value if f == 2 else value
                at = MASK - CUT + r
                ms[row] = jnp.broadcast_to(blocks[1][at : at + 1, :], (8, ZONAL))


def coriolis_table(fs, position, core, sign):
    offset = iota(fs.shape, 0) - HALO
    rows = position * BAND + jnp.where(core == 1, BAND - 1 - offset, offset)
    latitude = (rows.astype(F32) + 0.5) / float(EXTENT)
    latitude = jnp.where(latitude > 1.0, 2.0 - latitude, latitude)
    fs[...] = sign * (0.3 * (latitude - 0.5))


KEPT = 20


def inner_kernel(
    own_first, own_rest, mate_first, mate_rest, fold, coupling, depths, h_out, u_out, v_out, fold_out, hs, us, vs, ps, ms, fs
):
    core = core_index()
    sign = (1 - 2 * core).astype(F32)
    fields = (hs, us, vs)
    put_band(fields, ms, HALO, (own_first, own_rest), core, sign)
    put_band(fields, ms, HALO + BAND, (mate_first, mate_rest), core, sign)
    coriolis_table(fs, band_index(), core, sign)
    steps = fine_tools(fields, ps, ms, fs, coupling, depths)
    ends = [SPAN - 2 * t for t in range(FINE_STEPS)]
    steps([(HALO + 2 * t, (ends[t], ends[t] - 1, ends[t] - 2)) for t in range(FINE_STEPS)])
    fold_out[...] = fold[...].astype(F32)
    for out, field in zip((h_out, u_out, v_out), fields):
        out[...] = field[HALO : HALO + KEPT]


def outer_kernel(
    own_first, own_rest, other, h_in, u_in, v_in, fold, coupling, depths, vectors, following,
    fine, chunk, hs, us, vs, ps, ms, fs,
):
    position = band_index()
    core = core_index()
    sign = (1 - 2 * core).astype(F32)
    on_top = position == BANDS - 1
    fields = (hs, us, vs)
    for field, kept in zip(fields, (h_in, u_in, v_in)):
        field[HALO : HALO + KEPT] = kept[...]
    for r in range(BAND):
        row = HALO + r + core * (BAND - 1 - 2 * r)
        ms[row] = jnp.broadcast_to(own_rest[MASK - CUT + r : MASK - CUT + r + 1, :], (8, ZONAL))

    @pl.when(jnp.logical_not(on_top))
    def _():
        for k in range(BAND):
            for f in range(3 if k < BAND - 1 else 1):
                at = VELOCITY_AT[f] + LAYERS * k
                value = other[at : at + LAYERS, :].reshape(2, 8, ZONAL)
                fields[f][BAND - 1 - k] = sign * value if f == 2 else value
            ms[BAND - 1 - k] = jnp.broadcast_to(other[MASK_AT + k : MASK_AT + k + 1, :], (8, ZONAL))

    @pl.when(on_top)
    def _():
        index = jnp.broadcast_to(fold[...].astype(jnp.int32), (LAYERS, ZONAL))
        for r in range(BAND):
            for f in range(3):
                block, at = (own_first, f * 256 + r) if f < 2 else (own_rest, r)
                image = block[pl.ds(at, LAYERS, stride=BAND), :]
                image = jnp.take_along_axis(image, index, axis=1).reshape(2, 8, ZONAL)
                fields[f][r] = -image if f == 1 else image
            image = jnp.broadcast_to(own_rest[MASK - CUT + r : MASK - CUT + r + 1, :], (8, ZONAL))
            ms[r] = jnp.take_along_axis(image, index[:8], axis=1)

    coriolis_table(fs, position, core, sign)
    steps = fine_tools(fields, ps, ms, fs, coupling, depths)
    steps([(2 * t, (2 * t + 18, 2 * t + 17, 2 * t + 18)) for t in range(FINE_STEPS)])

    def row_of(r):
        return HALO + r + core * (BAND - 1 - 2 * r)

    root = jnp.sqrt(depths[...])
    jumps = []
    for f in range(3):
        rows = []
        for cr in range(4):
            here = [fields[f][row_of(4 * cr + r)].reshape(LAYERS, ZONAL) for r in range(4)]
            if f == 2:
                here = [sign * row for row in here]
            for r in range(4):
                fine[f * BAND + 4 * cr + r] = here[r]
            rows.append(here[0] + here[1] + here[2] + here[3])
        jumps.append(block_mean(rows) - following[f * LAYERS : (f + 1) * LAYERS, :])
    of_thickness = dot3(vectors[:, :LAYERS] / root, jumps[0])
    of_velocity = dot3(vectors[:, :LAYERS] * root, jnp.concatenate(jumps[1:], axis=1))
    for f, in_modes in enumerate((of_thickness, of_velocity[:, :ZONAL], of_velocity[:, ZONAL:])):
        chunk[pl.ds(f, LAYERS, stride=8), :] = in_modes
        chunk[pl.ds(4 + f, LAYERS, stride=8), :] = in_modes
    rows = []
    for cr in range(4):
        here = [ms[row_of(4 * cr + r)] for r in range(4)]
        rows.append(here[0] + here[1] + here[2] + here[3])
    chunk[pl.ds(3, BANDS, stride=4), :] = jnp.broadcast_to(block_mean(rows)[:1], (BANDS, ZONAL))


def coarse_tools(value, masks, fold):
    sub = iota((8, ZONAL), 0)
    lane = iota((8, ZONAL), 1)
    seg = lane % 4
    coriolis = []
    for cr in range(4):
        position = ((seg * 8 + sub) * 4 + cr).astype(F32)
        coriolis.append((4.0 * 0.3) * ((position + 0.5) / float(EXTENT // 4) - 0.5))
    keep = 1.0 - 4.0 * FRICTION
    k = fold[0, 0] // 4
    fold_index = 4 * ((k - lane // 4 + 32) % 32) + 3
    last, top = sub == 7, jnp.logical_and(sub == 7, seg == 3)
    first, bottom = sub == 0, jnp.logical_and(sub == 0, seg == 0)

    def east(x):
        return pltpu.roll(x, ZONAL - 4, 1) - pltpu.roll(x, 4, 1)

    def north(x, sign):
        up = pltpu.roll(x[0], 7, 0)
        up = jnp.where(last, pltpu.roll(up, ZONAL - 1, 1), up)
        up = jnp.where(top, sign * jnp.take_along_axis(x[3], fold_index, axis=1), up)
        down = pltpu.roll(x[3], 1, 0)
        down = jnp.where(first, pltpu.roll(down, 1, 1), down)
        down = jnp.where(bottom, 0.0, down)
        return [x[1] - down, x[2] - x[0], x[3] - x[1], up - x[2]]

    kept = [keep * m for m in masks]
    turned = [m * f for m, f in zip(masks, coriolis)]
    pushed = [(0.5 * value) * m for m in masks]
    spread = [0.5 * m for m in masks]

    def propagate(state):
        h, u, v = state
        for _ in range(2):
            north_h = north(h, 1.0)
            slow = [kept[i] * v[i] - pushed[i] * north_h[i] for i in range(4)]
            u = [(kept[i] * u[i] + turned[i] * v[i]) - pushed[i] * east(h[i]) for i in range(4)]
            v = [slow[i] - turned[i] * u[i] for i in range(4)]
            rest = [masks[i] * h[i] - spread[i] * east(u[i]) for i in range(4)]
            north_v = north(v, -1.0)
            h = [rest[i] - spread[i] * north_v[i] for i in range(4)]
        return [h, u, v]

    return propagate


def load_state(ref, begin=0):
    return [[ref[begin + f * 32 + cr * 8 : begin + f * 32 + cr * 8 + 8, :] for cr in range(4)] for f in range(3)]


def store_state(ref, state, begin=0):
    for f in range(3):
        for cr in range(4):
            ref[begin + f * 32 + cr * 8 : begin + f * 32 + cr * 8 + 8, :] = state[f][cr]


def add_state(a, b):
    return [[x + y for x, y in zip(p, q)] for p, q in zip(a, b)]


def load_masks(ref):
    return [ref[cr * 8 : cr * 8 + 8, :] for cr in range(4)]


PARTS = 7


def collect_kernel(spread, out):
    for core in range(2):

        @pl.when(core_index() == core)
        def _():
            for part in range(PARTS):
                at = core * 64 + part + (28 if part > 3 else 0)
                out[part * 8 : part * 8 + 8, :] = spread[pl.ds(at, 8, stride=4), :]


def pair_kernel(half, other_half, values, fold, jumps, mask_out, total):
    seg = iota((8, ZONAL), 1) % 4
    zh = lax.axis_index("zh")
    quarters = [(half, 0, zh), (half, PARTS * 8, zh ^ 1), (other_half, 0, zh ^ 3), (other_half, PARTS * 8, zh ^ 2)]
    for part in range(PARTS):
        rows = [None] * 4
        for ref, begin, quarter in quarters:
            piece = ref[begin + part * 8 : begin + part * 8 + 8, :]
            for cr in range(4):
                moved = pltpu.roll(piece, lax.rem(quarter - cr + ZONAL, ZONAL), 1)
                rows[cr] = moved if rows[cr] is None else jnp.where(seg == quarter, moved, rows[cr])
        for cr in range(4):
            if part == 3:
                mask_out[cr * 8 : cr * 8 + 8, :] = rows[cr]
            else:
                begin = (part if part < 3 else part - 1) * 32 + cr * 8
                jumps[begin : begin + 8, :] = rows[cr]
    propagate = coarse_tools(values[pl.ds(mode_index(), 1), :], load_masks(mask_out), fold)
    store_state(total, add_state(propagate(load_state(jumps)), load_state(jumps, 96)))


def group_kernel(total, mate, mask, values, fold, both):
    propagate = coarse_tools(values[pl.ds(mode_index(), 1), :], load_masks(mask), fold)
    odd = core_index() == 1
    mine, theirs = load_state(total), load_state(mate)
    earlier = [[jnp.where(odd, t, m) for m, t in zip(a, b)] for a, b in zip(mine, theirs)]
    later = [[jnp.where(odd, m, t) for m, t in zip(a, b)] for a, b in zip(mine, theirs)]
    trips = jnp.where(lax.axis_index("zl") < 3, 1, 0)
    state = lax.fori_loop(0, trips, lambda _, s: propagate(propagate(s)), earlier)
    store_state(both, add_state(state, later))


def repeat(wanted, propagate, state):
    return lax.fori_loop(0, jnp.where(wanted, 2, 0), lambda _, s: propagate(propagate(s)), state)


def earlier_kernel(three, mask, values, fold, out):
    propagate = coarse_tools(values[pl.ds(mode_index(), 1), :], load_masks(mask), fold)
    store_state(out, repeat(lax.axis_index("zl") == 3, propagate, load_state(three)))


def chain_kernel(one, two, earlier, mate, jumps, mask, values, fold, chunk):
    quarter = lax.axis_index("zh")
    core = core_index()
    propagate = coarse_tools(values[pl.ds(mode_index(), 1), :], load_masks(mask), fold)

    def twice(state):
        return propagate(propagate(state))

    state = add_state(load_state(earlier), load_state(two))
    state = repeat(lax.axis_index("zl") >= 2, propagate, state)
    state = add_state(state, load_state(one))
    state = lax.fori_loop(0, core, lambda _, s: add_state(twice(s), load_state(mate)), state)
    seg = iota((8, ZONAL), 1) % 4
    chunk[...] = jnp.zeros_like(chunk)
    for x in range(2):
        state = propagate(state)
        packed = []
        for f in range(3):
            pieces = [pltpu.roll(state[f][cr], lax.rem(cr - quarter + ZONAL, ZONAL), 1) for cr in range(4)]
            packed.append(pieces[0])
            for cr in range(1, 4):
                packed[f] = jnp.where(seg == cr, pieces[cr], packed[f])
        for which in range(2):

            @pl.when(core == which)
            def _():
                for f in range(3):
                    chunk[pl.ds((2 * which + x) * 32 + f, 8, stride=4), :] = packed[f]

        if x == 0:
            state = add_state(state, load_state(jumps))


def correct_kernel(fine, gathered, vectors, depths, out, result, sems):
    half = lax.axis_index("x") // 2
    lanes = jnp.broadcast_to(depths[...], (LAYERS, LAYERS))
    eye = iota((LAYERS, LAYERS), 0) == iota((LAYERS, LAYERS), 1)
    root = jnp.sqrt(jnp.sum(jnp.where(eye, lanes, 0.0), axis=1, keepdims=True))
    lane = iota((LAYERS, ZONAL), 1)
    copies = []
    for f in range(3):
        in_modes = jnp.where(
            half == 0, gathered[pl.ds(f, LAYERS, stride=8), :], gathered[pl.ds(4 + f, LAYERS, stride=8), :]
        )
        (top, rest), (mode_top, mode_rest) = two_parts(in_modes), two_parts(vectors[:, :LAYERS])
        change = lax.dot_general(
            jnp.concatenate([mode_top, mode_top, mode_rest], axis=0),
            jnp.concatenate([top, rest, top], axis=0),
            (((0,), (0,)), ((), ())), preferred_element_type=F32,
        )
        change = change * root if f == 0 else change / root
        for cr in range(4):
            spread = jnp.take_along_axis(change, lane // 4 * 4 + cr, axis=1)
            for r in range(4):
                row = 4 * cr + r
                result[pl.ds(f * 256 + row, LAYERS, stride=BAND), :] = fine[f * BAND + row] + spread
        here = pl.ds(f * 256, 256)
        copies.append(pltpu.make_async_copy(result.at[here], out.at[here], sems.at[f]))
        copies[-1].start()
    for copy in copies:
        copy.wait()


def call(kernel, out_shapes, scratch=(), spaces=None, out_space=pltpu.VMEM, flops=1 << 20, vmem=24 << 20):
    def run(*arrays):
        specs = [pl.BlockSpec(memory_space=s) for s in spaces or (pltpu.VMEM,) * len(arrays)]
        return pl.pallas_call(
            kernel,
            out_shape=[jax.ShapeDtypeStruct(s, F32) for s in out_shapes],
            in_specs=specs,
            out_specs=[pl.BlockSpec(memory_space=out_space)] * len(out_shapes),
            scratch_shapes=list(scratch),
            compiler_params=pltpu.CompilerParams(vmem_limit_bytes=vmem),
            cost_estimate=pl.CostEstimate(flops=flops, bytes_accessed=1 << 20, transcendentals=0),
        )(*arrays)

    return run


def swap(block, axes):
    return lax.all_to_all(block, axes, 0, 0, tiled=True)


def body(start_state, land_mask, fold_map, coupling, depths):
    sent, first, rest, restricted = call(
        pack_kernel,
        [(MASK_AT + BAND, ZONAL), (CUT, ZONAL), (MASK + BAND - CUT, ZONAL), (3 * LAYERS, ZONAL)],
        [pltpu.SemaphoreType.DMA((3,))],
        spaces=(pl.ANY, pl.ANY),
    )(start_state.reshape(MASK, ZONAL), land_mask.astype(F32))
    fold = fold_map.reshape(1, ZONAL)
    depth_row = depths.reshape(1, LAYERS)
    across = [(i, i + 1) for i in range(1, BANDS - 1, 2)]
    across += [(b, a) for a, b in across]
    other = lax.ppermute(sent, SPACE, across)
    following = lax.ppermute(restricted, TIME, [(n + 1, n) for n in range(15)])
    vectors, values = call(modes_kernel, [(LAYERS, ZONAL), (LAYERS, ZONAL)], flops=10 << 20)(
        coupling, depth_row
    )
    inside = [(i, i ^ 1) for i in range(BANDS)]
    mate = [lax.ppermute(part, SPACE, inside) for part in (first, rest)]

    state = pltpu.VMEM((SPAN, 2, 8, ZONAL), F32)
    table = pltpu.VMEM((SPAN, 8, ZONAL), F32)
    scratch = [state, state, state, state, table, table]
    *inner, fold_held = call(
        inner_kernel, [(KEPT, 2, 8, ZONAL)] * 3 + [(1, ZONAL)], scratch, flops=4 << 20
    )(first, rest, *mate, fold, coupling, depth_row)
    fine, chunk = call(
        outer_kernel, [(3 * BAND, LAYERS, ZONAL), (4 * BANDS, ZONAL)], scratch
    )(
        first, rest, other, *inner, fold_held, coupling, depth_row, vectors, following
    )

    spread = swap(chunk, PLANE)
    (mine,) = call(collect_kernel, [(PARTS * 8, ZONAL)])(spread)
    beside = lax.ppermute(mine, ("zh",), [(i, i ^ 1) for i in range(4)])
    half = jnp.concatenate([mine, beside], axis=0)
    other_half = lax.ppermute(half, ("zh",), [(i, i ^ 3) for i in range(4)])
    jumps, mask, total = call(
        pair_kernel, [(192, ZONAL), (32, ZONAL), (96, ZONAL)]
    )(half, other_half, values, fold)
    mate = lax.ppermute(total, ("c",), [(0, 1), (1, 0)])
    (both,) = call(group_kernel, [(96, ZONAL)])(total, mate, mask, values, fold)
    three, two, one = (
        lax.ppermute(both, ("zl",), [(i, i + d) for i in range(4 - d)]) for d in (3, 2, 1)
    )
    (earlier,) = call(earlier_kernel, [(96, ZONAL)])(three, mask, values, fold)
    (chunk,) = call(chain_kernel, [(4 * BANDS, ZONAL)])(
        one, two, earlier, mate, jumps, mask, values, fold
    )
    change = swap(chunk, PLANE)
    (result,) = call(
        correct_kernel,
        [(MASK, ZONAL)],
        [pltpu.VMEM((MASK, ZONAL), F32), pltpu.SemaphoreType.DMA((3,))],
        out_space=pl.ANY,
    )(
        fine, change, vectors, depth_row
    )
    return result.reshape(1, 3, LAYERS, BAND, ZONAL)


def solution(mesh):
    parts = Mesh(mesh.devices.reshape(4, 4, 4, 4, 2), ("zl", "x", "zh", "y", "c"))
    return jax.shard_map(
        body,
        mesh=parts,
        in_specs=(P(TIME, None, None, SPACE, None), P(SPACE, None), P(), P(), P()),
        out_specs=P(TIME, None, None, SPACE, None),
        check_vma=False,
    )
```

```python
import functools

import jax
import jax.numpy as jnp
from jax import lax
from jax.experimental import pallas as pl
from jax.experimental.pallas import tpu as pltpu
from jax.sharding import Mesh
from jax.sharding import PartitionSpec as P

LAYERS = 16
ZONAL = 128
FINE_STEPS = 8
BAND = 16
BANDS = 32
EXTENT = BAND * BANDS
HALO = 2 * FINE_STEPS
SPAN = BAND + 2 * HALO
FRICTION = 0.02
CUT = 2 * LAYERS * BAND
MASK = 3 * LAYERS * BAND
HIGHEST = lax.Precision.HIGHEST
F32 = jnp.float32
BF16 = jnp.bfloat16

SPACE = ("zh", "y", "c")
TIME = ("zl", "x")
PLANE = ("x", "y", "c")

SHIFT = 1.0


def iota(shape, axis):
    return lax.broadcasted_iota(jnp.int32, shape, axis)


def two_parts(x):
    top = x.astype(BF16)
    return top, (x - top.astype(F32)).astype(BF16)


def dot3(a, b):
    (a_top, a_rest), (b_top, b_rest) = two_parts(a), two_parts(b)
    left = jnp.concatenate([a_top, a_top, a_rest], axis=1)
    right = jnp.concatenate([b_top, b_rest, b_top], axis=0)
    return jnp.dot(left, right, preferred_element_type=F32)


def block_mean(rows):
    part = iota(rows[0].shape, 1) % 4

    def pairs(x, y, step):
        first = (part & step) == 0
        return jnp.where(first, x + pltpu.roll(x, ZONAL - step, 1), y + pltpu.roll(y, step, 1))

    return pairs(pairs(rows[0], rows[1], 1), pairs(rows[2], rows[3], 1), 2) * (1.0 / 16.0)


VELOCITY_AT = (0, LAYERS * BAND, LAYERS * (2 * BAND - 1))
MASK_AT = LAYERS * (3 * BAND - 2)


def pack_kernel(state, mask, sent, first, rest, restricted, sems):
    copies = [
        pltpu.make_async_copy(state.at[pl.ds(0, CUT)], first, sems.at[0]),
        pltpu.make_async_copy(state.at[pl.ds(CUT, MASK - CUT)], rest.at[pl.ds(0, MASK - CUT)], sems.at[1]),
        pltpu.make_async_copy(mask, rest.at[pl.ds(MASK - CUT, BAND)], sems.at[2]),
    ]
    for copy in copies:
        copy.start()
    for copy in copies:
        copy.wait()

    def row_of(f, r):
        if f < 2:
            return first[pl.ds(f * 256 + r, LAYERS, stride=BAND), :]
        return rest[pl.ds(r, LAYERS, stride=BAND), :]

    for odd in (False, True):

        @pl.when(core_index() == int(odd))
        def _():
            for k in range(BAND):
                r = BAND - 1 - k if odd else k
                for f in range(3 if k < BAND - 1 else 1):
                    at = VELOCITY_AT[f] + LAYERS * k
                    sent[at : at + LAYERS, :] = row_of(f, r)
                sent[MASK_AT + k : MASK_AT + k + 1, :] = rest[MASK - CUT + r : MASK - CUT + r + 1, :]

    for f in range(3):
        rows = []
        for cr in range(4):
            here = [row_of(f, 4 * cr + r) for r in range(4)]
            rows.append(here[0] + here[1] + here[2] + here[3])
        restricted[f * LAYERS : (f + 1) * LAYERS, :] = block_mean(rows)


def modes_kernel(coupling, depths, vectors, values):
    row = iota((LAYERS, ZONAL), 0)
    lane = iota((LAYERS, ZONAL), 1)
    eye = row == lane
    root = jnp.sqrt(depths[...])
    root = jnp.concatenate([root, jnp.zeros((1, ZONAL - LAYERS), F32)], axis=1)
    root_lanes = jnp.broadcast_to(root, (LAYERS, ZONAL))
    root_rows = jnp.sum(jnp.where(eye, root_lanes, 0.0), axis=1, keepdims=True)
    matrix = jnp.concatenate([coupling[...], jnp.zeros((LAYERS, ZONAL - LAYERS), F32)], axis=1)
    matrix = matrix * root_lanes * root_rows
    start = matrix + jnp.where(eye, SHIFT, 0.0) + jnp.where(lane == row + LAYERS, 1.0, 0.0)
    active = iota((8, ZONAL), 1) < LAYERS
    sub = iota((8, ZONAL), 0)

    def sums(x):
        return jnp.broadcast_to(jnp.sum(jnp.where(active, x, 0.0), axis=1, keepdims=True), x.shape)

    def turn(width, x):
        if width == 8:
            return pltpu.roll(x, 1, 0)
        return jnp.where((sub & (width - 1)) == 0, pltpu.roll(x, 9 - width, 0), pltpu.roll(x, 1, 0))

    def regroup(half, x, y):
        low = (sub & half) == 0
        return jnp.where(low, x, pltpu.roll(y, half, 0)), jnp.where(low, pltpu.roll(x, 8 - half, 0), y)

    def sweep(carry):
        count, _, x, y = carry
        xx, yy = sums(x * x), sums(y * y)
        worst = jnp.zeros((8, ZONAL), F32)
        for width in (8, 4, 2, 1):
            for _ in range(width):
                xy = sums(x * y)
                gap = yy - xx
                side = jnp.maximum(jnp.abs(gap), 1e-12)
                scale = lax.rsqrt(side * side + 4.0 * xy * xy)
                square = 0.5 + 0.5 * side * scale
                cosine_over = lax.rsqrt(square)
                signed = jnp.where(gap >= 0.0, xy, -xy) * scale
                cosine = square * cosine_over
                sine = signed * cosine_over
                tangent_xy = signed * xy / square
                worst = jnp.maximum(worst, jnp.abs(xy))
                x, y = cosine * x - sine * y, sine * x + cosine * y
                xx, yy = xx - tangent_xy, yy + tangent_xy
                if width > 1:
                    y, yy = turn(width, y), turn(width, yy)
            if width > 1:
                x, y = regroup(width // 2, x, y)
                xx, yy = regroup(width // 2, xx, yy)
        return count + 1, jnp.max(worst), x, y

    def unfinished(carry):
        return jnp.logical_and(carry[0] < 12, carry[1] > 2e-4)

    _, _, x, y = lax.while_loop(unfinished, sweep, (0, jnp.float32(1.0), start[:8], start[8:]))
    x = jnp.concatenate([x, y], axis=0)
    active = lane < LAYERS
    turned = pltpu.roll(x, ZONAL - LAYERS, 1)
    vectors[...] = jnp.where(active, turned, 0.0)
    value = jnp.sum(jnp.where(active, x * turned, 0.0), axis=1, keepdims=True) - SHIFT
    values[...] = jnp.broadcast_to(value, (LAYERS, ZONAL))


def east(x):
    flat = x.reshape(-1, ZONAL)
    return (pltpu.roll(flat, ZONAL - 1, 1) - pltpu.roll(flat, 1, 1)).reshape(x.shape)


def fine_tools(fields, ps, ms, fs, coupling, depths):
    hs, us, vs = fields
    half_top, half_rest = two_parts(0.5 * coupling[...])
    weights = jnp.concatenate([half_top, half_top, half_rest], axis=1)
    lanes = jnp.broadcast_to(depths[...], (LAYERS, LAYERS))
    eye = iota((LAYERS, LAYERS), 0) == iota((LAYERS, LAYERS), 1)
    thick = 0.5 * jnp.sum(jnp.where(eye, lanes, 0.0), axis=1, keepdims=True)
    thick = jnp.broadcast_to(thick, (LAYERS, ZONAL)).reshape(1, 2, 8, ZONAL)
    keep = 1.0 - FRICTION

    def pressure(low, high):
        wide = jnp.concatenate([hs[j].reshape(LAYERS, ZONAL) for j in range(low, high)], axis=1)
        top, rest = two_parts(wide)
        stacked = jnp.concatenate([top, rest, top], axis=0)
        result = jnp.dot(weights, stacked, preferred_element_type=F32)
        for j in range(low, high):
            ps[j] = result[:, (j - low) * ZONAL : (j - low + 1) * ZONAL].reshape(2, 8, ZONAL)

    def velocity(low, high):
        m = ms[low:high][:, None]
        f = fs[low:high][:, None]
        u = us[low:high]
        v = vs[low:high]
        u = m * (keep * u + f * v - east(ps[low:high]))
        v = m * (keep * v - f * u - (ps[low + 1 : high + 1] - ps[low - 1 : high - 1]))
        us[low:high] = u
        vs[low:high] = v

    def thickness(low, high):
        m = ms[low:high][:, None]
        spread = east(us[low:high]) + (vs[low + 1 : high + 1] - vs[low - 1 : high - 1])
        hs[low:high] = m * (hs[low:high] - thick * spread)

    def steps(bounds):
        for low, ends in bounds:
            for at in range(low, ends[0], 4):
                pressure(at, min(at + 4, ends[0]))
            for at in range(low + 1, ends[1], 4):
                velocity(at, min(at + 4, ends[1]))
            for at in range(low + 2, ends[2], 4):
                thickness(at, min(at + 4, ends[2]))

    return steps


def core_index():
    return lax.axis_index("c")


def band_index():
    return lax.axis_index("zh") * 8 + lax.axis_index("y") * 2 + lax.axis_index("c")


def mode_index():
    return lax.axis_index("x") * 4 + lax.axis_index("y")


def put_band(fields, ms, begin, blocks, core, sign):
    for odd in (False, True):

        @pl.when(core == int(odd))
        def _():
            for r in range(BAND):
                row = begin + (BAND - 1 - r if odd else r)
                for f in range(3):
                    at = f * 256 + r - (CUT if f == 2 else 0)
                    value = blocks[f // 2][pl.ds(at, LAYERS, stride=BAND), :].reshape(2, 8, ZONAL)
                    fields[f][row] = sign * value if f == 2 else value
                at = MASK - CUT + r
                ms[row] = jnp.broadcast_to(blocks[1][at : at + 1, :], (8, ZONAL))


def coriolis_table(fs, position, core, sign):
    offset = iota(fs.shape, 0) - HALO
    rows = position * BAND + jnp.where(core == 1, BAND - 1 - offset, offset)
    latitude = (rows.astype(F32) + 0.5) / float(EXTENT)
    latitude = jnp.where(latitude > 1.0, 2.0 - latitude, latitude)
    fs[...] = sign * (0.3 * (latitude - 0.5))


KEPT = 20


def inner_kernel(
    own_first, own_rest, mate_first, mate_rest, fold, coupling, depths, h_out, u_out, v_out, fold_out, hs, us, vs, ps, ms, fs
):
    core = core_index()
    sign = (1 - 2 * core).astype(F32)
    fields = (hs, us, vs)
    put_band(fields, ms, HALO, (own_first, own_rest), core, sign)
    put_band(fields, ms, HALO + BAND, (mate_first, mate_rest), core, sign)
    coriolis_table(fs, band_index(), core, sign)
    steps = fine_tools(fields, ps, ms, fs, coupling, depths)
    ends = [SPAN - 2 * t for t in range(FINE_STEPS)]
    steps([(HALO + 2 * t, (ends[t], ends[t] - 1, ends[t] - 2)) for t in range(FINE_STEPS)])
    fold_out[...] = fold[...].astype(F32)
    for out, field in zip((h_out, u_out, v_out), fields):
        out[...] = field[HALO : HALO + KEPT]


def outer_kernel(
    own_first, own_rest, other, h_in, u_in, v_in, fold, coupling, depths, vectors, following,
    fine, chunk, hs, us, vs, ps, ms, fs,
):
    position = band_index()
    core = core_index()
    sign = (1 - 2 * core).astype(F32)
    on_top = position == BANDS - 1
    fields = (hs, us, vs)
    for field, kept in zip(fields, (h_in, u_in, v_in)):
        field[HALO : HALO + KEPT] = kept[...]
    for r in range(BAND):
        row = HALO + r + core * (BAND - 1 - 2 * r)
        ms[row] = jnp.broadcast_to(own_rest[MASK - CUT + r : MASK - CUT + r + 1, :], (8, ZONAL))

    @pl.when(jnp.logical_not(on_top))
    def _():
        for k in range(BAND):
            for f in range(3 if k < BAND - 1 else 1):
                at = VELOCITY_AT[f] + LAYERS * k
                value = other[at : at + LAYERS, :].reshape(2, 8, ZONAL)
                fields[f][BAND - 1 - k] = sign * value if f == 2 else value
            ms[BAND - 1 - k] = jnp.broadcast_to(other[MASK_AT + k : MASK_AT + k + 1, :], (8, ZONAL))

    @pl.when(on_top)
    def _():
        index = jnp.broadcast_to(fold[...].astype(jnp.int32), (LAYERS, ZONAL))
        for r in range(BAND):
            for f in range(3):
                block, at = (own_first, f * 256 + r) if f < 2 else (own_rest, r)
                image = block[pl.ds(at, LAYERS, stride=BAND), :]
                image = jnp.take_along_axis(image, index, axis=1).reshape(2, 8, ZONAL)
                fields[f][r] = -image if f == 1 else image
            image = jnp.broadcast_to(own_rest[MASK - CUT + r : MASK - CUT + r + 1, :], (8, ZONAL))
            ms[r] = jnp.take_along_axis(image, index[:8], axis=1)

    coriolis_table(fs, position, core, sign)
    steps = fine_tools(fields, ps, ms, fs, coupling, depths)
    steps([(2 * t, (2 * t + 18, 2 * t + 17, 2 * t + 18)) for t in range(FINE_STEPS)])

    def row_of(r):
        return HALO + r + core * (BAND - 1 - 2 * r)

    root = jnp.sqrt(depths[...])
    jumps = []
    for f in range(3):
        rows = []
        for cr in range(4):
            here = [fields[f][row_of(4 * cr + r)].reshape(LAYERS, ZONAL) for r in range(4)]
            if f == 2:
                here = [sign * row for row in here]
            for r in range(4):
                fine[f * BAND + 4 * cr + r] = here[r]
            rows.append(here[0] + here[1] + here[2] + here[3])
        jumps.append(block_mean(rows) - following[f * LAYERS : (f + 1) * LAYERS, :])
    of_thickness = dot3(vectors[:, :LAYERS] / root, jumps[0])
    of_velocity = dot3(vectors[:, :LAYERS] * root, jnp.concatenate(jumps[1:], axis=1))
    for f, in_modes in enumerate((of_thickness, of_velocity[:, :ZONAL], of_velocity[:, ZONAL:])):
        chunk[pl.ds(f, LAYERS, stride=8), :] = in_modes
        chunk[pl.ds(4 + f, LAYERS, stride=8), :] = in_modes
    rows = []
    for cr in range(4):
        here = [ms[row_of(4 * cr + r)] for r in range(4)]
        rows.append(here[0] + here[1] + here[2] + here[3])
    chunk[pl.ds(3, BANDS, stride=4), :] = jnp.broadcast_to(block_mean(rows)[:1], (BANDS, ZONAL))


def coarse_tools(value, masks, fold):
    sub = iota((8, ZONAL), 0)
    lane = iota((8, ZONAL), 1)
    seg = lane % 4
    coriolis = []
    for cr in range(4):
        position = ((seg * 8 + sub) * 4 + cr).astype(F32)
        coriolis.append((4.0 * 0.3) * ((position + 0.5) / float(EXTENT // 4) - 0.5))
    keep = 1.0 - 4.0 * FRICTION
    k = fold[0, 0] // 4
    fold_index = 4 * ((k - lane // 4 + 32) % 32) + 3
    last, top = sub == 7, jnp.logical_and(sub == 7, seg == 3)
    first, bottom = sub == 0, jnp.logical_and(sub == 0, seg == 0)

    def east(x):
        return pltpu.roll(x, ZONAL - 4, 1) - pltpu.roll(x, 4, 1)

    def north(x, sign):
        up = pltpu.roll(x[0], 7, 0)
        up = jnp.where(last, pltpu.roll(up, ZONAL - 1, 1), up)
        up = jnp.where(top, sign * jnp.take_along_axis(x[3], fold_index, axis=1), up)
        down = pltpu.roll(x[3], 1, 0)
        down = jnp.where(first, pltpu.roll(down, 1, 1), down)
        down = jnp.where(bottom, 0.0, down)
        return [x[1] - down, x[2] - x[0], x[3] - x[1], up - x[2]]

    kept = [keep * m for m in masks]
    turned = [m * f for m, f in zip(masks, coriolis)]
    pushed = [(0.5 * value) * m for m in masks]
    spread = [0.5 * m for m in masks]

    def propagate(state):
        h, u, v = state
        for _ in range(2):
            north_h = north(h, 1.0)
            slow = [kept[i] * v[i] - pushed[i] * north_h[i] for i in range(4)]
            u = [(kept[i] * u[i] + turned[i] * v[i]) - pushed[i] * east(h[i]) for i in range(4)]
            v = [slow[i] - turned[i] * u[i] for i in range(4)]
            rest = [masks[i] * h[i] - spread[i] * east(u[i]) for i in range(4)]
            north_v = north(v, -1.0)
            h = [rest[i] - spread[i] * north_v[i] for i in range(4)]
        return [h, u, v]

    return propagate


def load_state(ref, begin=0):
    return [[ref[begin + f * 32 + cr * 8 : begin + f * 32 + cr * 8 + 8, :] for cr in range(4)] for f in range(3)]


def store_state(ref, state, begin=0):
    for f in range(3):
        for cr in range(4):
            ref[begin + f * 32 + cr * 8 : begin + f * 32 + cr * 8 + 8, :] = state[f][cr]


def add_state(a, b):
    return [[x + y for x, y in zip(p, q)] for p, q in zip(a, b)]


def load_masks(ref):
    return [ref[cr * 8 : cr * 8 + 8, :] for cr in range(4)]


PARTS = 7


def collect_kernel(spread, out):
    for core in range(2):

        @pl.when(core_index() == core)
        def _():
            for part in range(PARTS):
                at = core * 64 + part + (28 if part > 3 else 0)
                out[part * 8 : part * 8 + 8, :] = spread[pl.ds(at, 8, stride=4), :]


def pair_kernel(half, other_half, values, fold, jumps, mask_out, total):
    seg = iota((8, ZONAL), 1) % 4
    zh = lax.axis_index("zh")
    quarters = [(half, 0, zh), (half, PARTS * 8, zh ^ 3), (other_half, 0, zh ^ 1), (other_half, PARTS * 8, zh ^ 2)]
    for part in range(PARTS):
        rows = [None] * 4
        for ref, begin, quarter in quarters:
            piece = ref[begin + part * 8 : begin + part * 8 + 8, :]
            for cr in range(4):
                moved = pltpu.roll(piece, lax.rem(quarter - cr + ZONAL, ZONAL), 1)
                rows[cr] = moved if rows[cr] is None else jnp.where(seg == quarter, moved, rows[cr])
        for cr in range(4):
            if part == 3:
                mask_out[cr * 8 : cr * 8 + 8, :] = rows[cr]
            else:
                begin = (part if part < 3 else part - 1) * 32 + cr * 8
                jumps[begin : begin + 8, :] = rows[cr]
    propagate = coarse_tools(values[pl.ds(mode_index(), 1), :], load_masks(mask_out), fold)
    store_state(total, add_state(propagate(load_state(jumps)), load_state(jumps, 96)))


def group_kernel(total, mate, mask, values, fold, both):
    propagate = coarse_tools(values[pl.ds(mode_index(), 1), :], load_masks(mask), fold)
    odd = core_index() == 1
    mine, theirs = load_state(total), load_state(mate)
    earlier = [[jnp.where(odd, t, m) for m, t in zip(a, b)] for a, b in zip(mine, theirs)]
    later = [[jnp.where(odd, m, t) for m, t in zip(a, b)] for a, b in zip(mine, theirs)]
    trips = jnp.where(lax.axis_index("zl") < 3, 1, 0)
    state = lax.fori_loop(0, trips, lambda _, s: propagate(propagate(s)), earlier)
    store_state(both, add_state(state, later))


def repeat(wanted, propagate, state):
    return lax.fori_loop(0, jnp.where(wanted, 2, 0), lambda _, s: propagate(propagate(s)), state)


def earlier_kernel(three, mask, values, fold, out):
    propagate = coarse_tools(values[pl.ds(mode_index(), 1), :], load_masks(mask), fold)
    store_state(out, repeat(lax.axis_index("zl") == 3, propagate, load_state(three)))


def chain_kernel(one, two, earlier, mate, jumps, mask, values, fold, chunk):
    quarter = lax.axis_index("zh")
    core = core_index()
    propagate = coarse_tools(values[pl.ds(mode_index(), 1), :], load_masks(mask), fold)

    def twice(state):
        return propagate(propagate(state))

    state = add_state(load_state(earlier), load_state(two))
    state = repeat(lax.axis_index("zl") >= 2, propagate, state)
    state = add_state(state, load_state(one))
    state = lax.fori_loop(0, core, lambda _, s: add_state(twice(s), load_state(mate)), state)
    seg = iota((8, ZONAL), 1) % 4
    chunk[...] = jnp.zeros_like(chunk)
    for x in range(2):
        state = propagate(state)
        packed = []
        for f in range(3):
            pieces = [pltpu.roll(state[f][cr], lax.rem(cr - quarter + ZONAL, ZONAL), 1) for cr in range(4)]
            packed.append(pieces[0])
            for cr in range(1, 4):
                packed[f] = jnp.where(seg == cr, pieces[cr], packed[f])
        for which in range(2):

            @pl.when(core == which)
            def _():
                for f in range(3):
                    chunk[pl.ds((2 * which + x) * 32 + f, 8, stride=4), :] = packed[f]

        if x == 0:
            state = add_state(state, load_state(jumps))


def correct_kernel(fine, gathered, vectors, depths, out, result, sems):
    half = lax.axis_index("x") // 2
    lanes = jnp.broadcast_to(depths[...], (LAYERS, LAYERS))
    eye = iota((LAYERS, LAYERS), 0) == iota((LAYERS, LAYERS), 1)
    root = jnp.sqrt(jnp.sum(jnp.where(eye, lanes, 0.0), axis=1, keepdims=True))
    lane = iota((LAYERS, ZONAL), 1)
    copies = []
    for f in range(3):
        in_modes = jnp.where(
            half == 0, gathered[pl.ds(f, LAYERS, stride=8), :], gathered[pl.ds(4 + f, LAYERS, stride=8), :]
        )
        (top, rest), (mode_top, mode_rest) = two_parts(in_modes), two_parts(vectors[:, :LAYERS])
        change = lax.dot_general(
            jnp.concatenate([mode_top, mode_top, mode_rest], axis=0),
            jnp.concatenate([top, rest, top], axis=0),
            (((0,), (0,)), ((), ())), preferred_element_type=F32,
        )
        change = change * root if f == 0 else change / root
        for cr in range(4):
            spread = jnp.take_along_axis(change, lane // 4 * 4 + cr, axis=1)
            for r in range(4):
                row = 4 * cr + r
                result[pl.ds(f * 256 + row, LAYERS, stride=BAND), :] = fine[f * BAND + row] + spread
        here = pl.ds(f * 256, 256)
        copies.append(pltpu.make_async_copy(result.at[here], out.at[here], sems.at[f]))
        copies[-1].start()
    for copy in copies:
        copy.wait()


def call(kernel, out_shapes, scratch=(), spaces=None, out_space=pltpu.VMEM, flops=1 << 20, vmem=24 << 20):
    def run(*arrays):
        specs = [pl.BlockSpec(memory_space=s) for s in spaces or (pltpu.VMEM,) * len(arrays)]
        return pl.pallas_call(
            kernel,
            out_shape=[jax.ShapeDtypeStruct(s, F32) for s in out_shapes],
            in_specs=specs,
            out_specs=[pl.BlockSpec(memory_space=out_space)] * len(out_shapes),
            scratch_shapes=list(scratch),
            compiler_params=pltpu.CompilerParams(vmem_limit_bytes=vmem),
            cost_estimate=pl.CostEstimate(flops=flops, bytes_accessed=1 << 20, transcendentals=0),
        )(*arrays)

    return run


def swap(block, axes):
    return lax.all_to_all(block, axes, 0, 0, tiled=True)


def body(start_state, land_mask, fold_map, coupling, depths):
    sent, first, rest, restricted = call(
        pack_kernel,
        [(MASK_AT + BAND, ZONAL), (CUT, ZONAL), (MASK + BAND - CUT, ZONAL), (3 * LAYERS, ZONAL)],
        [pltpu.SemaphoreType.DMA((3,))],
        spaces=(pl.ANY, pl.ANY),
    )(start_state.reshape(MASK, ZONAL), land_mask.astype(F32))
    fold = fold_map.reshape(1, ZONAL)
    depth_row = depths.reshape(1, LAYERS)
    across = [(i, i + 1) for i in range(1, BANDS - 1, 2)]
    across += [(b, a) for a, b in across]
    other = lax.ppermute(sent, SPACE, across)
    following = lax.ppermute(restricted, TIME, [(n + 1, n) for n in range(15)])
    vectors, values = call(modes_kernel, [(LAYERS, ZONAL), (LAYERS, ZONAL)], flops=10 << 20)(
        coupling, depth_row
    )
    inside = [(i, i ^ 1) for i in range(BANDS)]
    mate = [lax.ppermute(part, SPACE, inside) for part in (first, rest)]

    state = pltpu.VMEM((SPAN, 2, 8, ZONAL), F32)
    table = pltpu.VMEM((SPAN, 8, ZONAL), F32)
    scratch = [state, state, state, state, table, table]
    *inner, fold_held = call(
        inner_kernel, [(KEPT, 2, 8, ZONAL)] * 3 + [(1, ZONAL)], scratch, flops=4 << 20
    )(first, rest, *mate, fold, coupling, depth_row)
    fine, chunk = call(
        outer_kernel, [(3 * BAND, LAYERS, ZONAL), (4 * BANDS, ZONAL)], scratch
    )(
        first, rest, other, *inner, fold_held, coupling, depth_row, vectors, following
    )

    spread = swap(chunk, PLANE)
    (mine,) = call(collect_kernel, [(PARTS * 8, ZONAL)])(spread)
    beside = lax.ppermute(mine, ("zh",), [(i, i ^ 3) for i in range(4)])
    half = jnp.concatenate([mine, beside], axis=0)
    other_half = lax.ppermute(half, ("zh",), [(i, i ^ 1) for i in range(4)])
    jumps, mask, total = call(
        pair_kernel, [(192, ZONAL), (32, ZONAL), (96, ZONAL)]
    )(half, other_half, values, fold)
    mate = lax.ppermute(total, ("c",), [(0, 1), (1, 0)])
    (both,) = call(group_kernel, [(96, ZONAL)])(total, mate, mask, values, fold)
    three, two, one = (
        lax.ppermute(both, ("zl",), [(i, i + d) for i in range(4 - d)]) for d in (3, 2, 1)
    )
    (earlier,) = call(earlier_kernel, [(96, ZONAL)])(three, mask, values, fold)
    (chunk,) = call(chain_kernel, [(4 * BANDS, ZONAL)])(
        one, two, earlier, mate, jumps, mask, values, fold
    )
    change = swap(chunk, PLANE)
    (result,) = call(
        correct_kernel,
        [(MASK, ZONAL)],
        [pltpu.VMEM((MASK, ZONAL), F32), pltpu.SemaphoreType.DMA((3,))],
        out_space=pl.ANY,
    )(
        fine, change, vectors, depth_row
    )
    return result.reshape(1, 3, LAYERS, BAND, ZONAL)


def solution(mesh):
    parts = Mesh(mesh.devices.reshape(4, 4, 4, 4, 2), ("zl", "x", "zh", "y", "c"))
    return jax.shard_map(
        body,
        mesh=parts,
        in_specs=(P(TIME, None, None, SPACE, None), P(SPACE, None), P(), P(), P()),
        out_specs=P(TIME, None, None, SPACE, None),
        check_vma=False,
    )
```

```python
import functools

import jax
import jax.numpy as jnp
from jax import lax
from jax.experimental import pallas as pl
from jax.experimental.pallas import tpu as pltpu
from jax.sharding import Mesh
from jax.sharding import PartitionSpec as P

LAYERS = 16
ZONAL = 128
FINE_STEPS = 8
BAND = 16
BANDS = 32
EXTENT = BAND * BANDS
HALO = 2 * FINE_STEPS
SPAN = BAND + 2 * HALO
FRICTION = 0.02
CUT = 2 * LAYERS * BAND
MASK = 3 * LAYERS * BAND
HIGHEST = lax.Precision.HIGHEST
F32 = jnp.float32
BF16 = jnp.bfloat16

SPACE = ("zh", "y", "c")
TIME = ("zl", "x")
PLANE = ("x", "y", "c")

SHIFT = 1.0


def iota(shape, axis):
    return lax.broadcasted_iota(jnp.int32, shape, axis)


def two_parts(x):
    top = x.astype(BF16)
    return top, (x - top.astype(F32)).astype(BF16)


def dot3(a, b):
    (a_top, a_rest), (b_top, b_rest) = two_parts(a), two_parts(b)
    left = jnp.concatenate([a_top, a_top, a_rest], axis=1)
    right = jnp.concatenate([b_top, b_rest, b_top], axis=0)
    return jnp.dot(left, right, preferred_element_type=F32)


def block_mean(rows):
    part = iota(rows[0].shape, 1) % 4

    def pairs(x, y, step):
        first = (part & step) == 0
        return jnp.where(first, x + pltpu.roll(x, ZONAL - step, 1), y + pltpu.roll(y, step, 1))

    return pairs(pairs(rows[0], rows[1], 1), pairs(rows[2], rows[3], 1), 2) * (1.0 / 16.0)


VELOCITY_AT = (0, LAYERS * BAND, LAYERS * (2 * BAND - 1))
MASK_AT = LAYERS * (3 * BAND - 2)


def pack_kernel(state, mask, sent, first, rest, restricted, sems):
    copies = [
        pltpu.make_async_copy(state.at[pl.ds(0, CUT)], first, sems.at[0]),
        pltpu.make_async_copy(state.at[pl.ds(CUT, MASK - CUT)], rest.at[pl.ds(0, MASK - CUT)], sems.at[1]),
        pltpu.make_async_copy(mask, rest.at[pl.ds(MASK - CUT, BAND)], sems.at[2]),
    ]
    for copy in copies:
        copy.start()
    for copy in copies:
        copy.wait()

    def row_of(f, r):
        if f < 2:
            return first[pl.ds(f * 256 + r, LAYERS, stride=BAND), :]
        return rest[pl.ds(r, LAYERS, stride=BAND), :]

    for odd in (False, True):

        @pl.when(core_index() == int(odd))
        def _():
            for k in range(BAND):
                r = BAND - 1 - k if odd else k
                for f in range(3 if k < BAND - 1 else 1):
                    at = VELOCITY_AT[f] + LAYERS * k
                    sent[at : at + LAYERS, :] = row_of(f, r)
                sent[MASK_AT + k : MASK_AT + k + 1, :] = rest[MASK - CUT + r : MASK - CUT + r + 1, :]

    for f in range(3):
        rows = []
        for cr in range(4):
            here = [row_of(f, 4 * cr + r) for r in range(4)]
            rows.append(here[0] + here[1] + here[2] + here[3])
        restricted[f * LAYERS : (f + 1) * LAYERS, :] = block_mean(rows)


def modes_kernel(coupling, depths, vectors, values):
    row = iota((LAYERS, ZONAL), 0)
    lane = iota((LAYERS, ZONAL), 1)
    eye = row == lane
    root = jnp.sqrt(depths[...])
    root = jnp.concatenate([root, jnp.zeros((1, ZONAL - LAYERS), F32)], axis=1)
    root_lanes = jnp.broadcast_to(root, (LAYERS, ZONAL))
    root_rows = jnp.sum(jnp.where(eye, root_lanes, 0.0), axis=1, keepdims=True)
    matrix = jnp.concatenate([coupling[...], jnp.zeros((LAYERS, ZONAL - LAYERS), F32)], axis=1)
    matrix = matrix * root_lanes * root_rows
    start = matrix + jnp.where(eye, SHIFT, 0.0) + jnp.where(lane == row + LAYERS, 1.0, 0.0)
    active = iota((8, ZONAL), 1) < LAYERS
    sub = iota((8, ZONAL), 0)

    def sums(x):
        return jnp.broadcast_to(jnp.sum(jnp.where(active, x, 0.0), axis=1, keepdims=True), x.shape)

    def turn(width, x):
        if width == 8:
            return pltpu.roll(x, 1, 0)
        return jnp.where((sub & (width - 1)) == 0, pltpu.roll(x, 9 - width, 0), pltpu.roll(x, 1, 0))

    def regroup(half, x, y):
        low = (sub & half) == 0
        return jnp.where(low, x, pltpu.roll(y, half, 0)), jnp.where(low, pltpu.roll(x, 8 - half, 0), y)

    def sweep(carry):
        count, _, x, y = carry
        xx, yy = sums(x * x), sums(y * y)
        worst = jnp.zeros((8, ZONAL), F32)
        for width in (8, 4, 2, 1):
            for _ in range(width):
                xy = sums(x * y)
                gap = yy - xx
                side = jnp.maximum(jnp.abs(gap), 1e-12)
                scale = lax.rsqrt(side * side + 4.0 * xy * xy)
                square = 0.5 + 0.5 * side * scale
                cosine_over = lax.rsqrt(square)
                signed = jnp.where(gap >= 0.0, xy, -xy) * scale
                cosine = square * cosine_over
                sine = signed * cosine_over
                tangent_xy = signed * xy / square
                worst = jnp.maximum(worst, jnp.abs(xy))
                x, y = cosine * x - sine * y, sine * x + cosine * y
                xx, yy = xx - tangent_xy, yy + tangent_xy
                if width > 1:
                    y, yy = turn(width, y), turn(width, yy)
            if width > 1:
                x, y = regroup(width // 2, x, y)
                xx, yy = regroup(width // 2, xx, yy)
        return count + 1, jnp.max(worst), x, y

    def unfinished(carry):
        return jnp.logical_and(carry[0] < 12, carry[1] > 2e-4)

    _, _, x, y = lax.while_loop(unfinished, sweep, (0, jnp.float32(1.0), start[:8], start[8:]))
    x = jnp.concatenate([x, y], axis=0)
    active = lane < LAYERS
    turned = pltpu.roll(x, ZONAL - LAYERS, 1)
    vectors[...] = jnp.where(active, turned, 0.0)
    value = jnp.sum(jnp.where(active, x * turned, 0.0), axis=1, keepdims=True) - SHIFT
    values[...] = jnp.broadcast_to(value, (LAYERS, ZONAL))


def east(x):
    flat = x.reshape(-1, ZONAL)
    return (pltpu.roll(flat, ZONAL - 1, 1) - pltpu.roll(flat, 1, 1)).reshape(x.shape)


def fine_tools(fields, ps, ms, fs, coupling, depths):
    hs, us, vs = fields
    half_top, half_rest = two_parts(0.5 * coupling[...])
    weights = jnp.concatenate([half_top, half_top, half_rest], axis=1)
    lanes = jnp.broadcast_to(depths[...], (LAYERS, LAYERS))
    eye = iota((LAYERS, LAYERS), 0) == iota((LAYERS, LAYERS), 1)
    thick = 0.5 * jnp.sum(jnp.where(eye, lanes, 0.0), axis=1, keepdims=True)
    thick = jnp.broadcast_to(thick, (LAYERS, ZONAL)).reshape(1, 2, 8, ZONAL)
    keep = 1.0 - FRICTION

    def pressure(low, high):
        wide = jnp.concatenate([hs[j].reshape(LAYERS, ZONAL) for j in range(low, high)], axis=1)
        top, rest = two_parts(wide)
        stacked = jnp.concatenate([top, rest, top], axis=0)
        result = jnp.dot(weights, stacked, preferred_element_type=F32)
        for j in range(low, high):
            ps[j] = result[:, (j - low) * ZONAL : (j - low + 1) * ZONAL].reshape(2, 8, ZONAL)

    def velocity(low, high):
        m = ms[low:high][:, None]
        f = fs[low:high][:, None]
        u = us[low:high]
        v = vs[low:high]
        u = m * (keep * u + f * v - east(ps[low:high]))
        v = m * (keep * v - f * u - (ps[low + 1 : high + 1] - ps[low - 1 : high - 1]))
        us[low:high] = u
        vs[low:high] = v

    def thickness(low, high):
        m = ms[low:high][:, None]
        spread = east(us[low:high]) + (vs[low + 1 : high + 1] - vs[low - 1 : high - 1])
        hs[low:high] = m * (hs[low:high] - thick * spread)

    def steps(bounds):
        for low, ends in bounds:
            for at in range(low, ends[0], 4):
                pressure(at, min(at + 4, ends[0]))
            for at in range(low + 1, ends[1], 4):
                velocity(at, min(at + 4, ends[1]))
            for at in range(low + 2, ends[2], 4):
                thickness(at, min(at + 4, ends[2]))

    return steps


def core_index():
    return lax.axis_index("c")


def band_index():
    return lax.axis_index("zh") * 8 + lax.axis_index("y") * 2 + lax.axis_index("c")


def mode_index():
    return lax.axis_index("x") * 4 + lax.axis_index("y")


def put_band(fields, ms, begin, blocks, core, sign):
    for odd in (False, True):

        @pl.when(core == int(odd))
        def _():
            for r in range(BAND):
                row = begin + (BAND - 1 - r if odd else r)
                for f in range(3):
                    at = f * 256 + r - (CUT if f == 2 else 0)
                    value = blocks[f // 2][pl.ds(at, LAYERS, stride=BAND), :].reshape(2, 8, ZONAL)
                    fields[f][row] = sign * value if f == 2 else value
                at = MASK - CUT + r
                ms[row] = jnp.broadcast_to(blocks[1][at : at + 1, :], (8, ZONAL))


def coriolis_table(fs, position, core, sign):
    offset = iota(fs.shape, 0) - HALO
    rows = position * BAND + jnp.where(core == 1, BAND - 1 - offset, offset)
    latitude = (rows.astype(F32) + 0.5) / float(EXTENT)
    latitude = jnp.where(latitude > 1.0, 2.0 - latitude, latitude)
    fs[...] = sign * (0.3 * (latitude - 0.5))


KEPT = 20


def inner_kernel(
    own_first, own_rest, mate_first, mate_rest, fold, coupling, depths, h_out, u_out, v_out, fold_out, hs, us, vs, ps, ms, fs
):
    core = core_index()
    sign = (1 - 2 * core).astype(F32)
    fields = (hs, us, vs)
    put_band(fields, ms, HALO, (own_first, own_rest), core, sign)
    put_band(fields, ms, HALO + BAND, (mate_first, mate_rest), core, sign)
    coriolis_table(fs, band_index(), core, sign)
    steps = fine_tools(fields, ps, ms, fs, coupling, depths)
    ends = [SPAN - 2 * t for t in range(FINE_STEPS)]
    steps([(HALO + 2 * t, (ends[t], ends[t] - 1, ends[t] - 2)) for t in range(FINE_STEPS)])
    fold_out[...] = fold[...].astype(F32)
    for out, field in zip((h_out, u_out, v_out), fields):
        out[...] = field[HALO : HALO + KEPT]


def outer_kernel(
    own_first, own_rest, other, h_in, u_in, v_in, fold, coupling, depths, vectors, following,
    fine, chunk, hs, us, vs, ps, ms, fs,
):
    position = band_index()
    core = core_index()
    sign = (1 - 2 * core).astype(F32)
    on_top = position == BANDS - 1
    fields = (hs, us, vs)
    for field, kept in zip(fields, (h_in, u_in, v_in)):
        field[HALO : HALO + KEPT] = kept[...]
    for r in range(BAND):
        row = HALO + r + core * (BAND - 1 - 2 * r)
        ms[row] = jnp.broadcast_to(own_rest[MASK - CUT + r : MASK - CUT + r + 1, :], (8, ZONAL))

    @pl.when(jnp.logical_not(on_top))
    def _():
        for k in range(BAND):
            for f in range(3 if k < BAND - 1 else 1):
                at = VELOCITY_AT[f] + LAYERS * k
                value = other[at : at + LAYERS, :].reshape(2, 8, ZONAL)
                fields[f][BAND - 1 - k] = sign * value if f == 2 else value
            ms[BAND - 1 - k] = jnp.broadcast_to(other[MASK_AT + k : MASK_AT + k + 1, :], (8, ZONAL))

    @pl.when(on_top)
    def _():
        index = jnp.broadcast_to(fold[...].astype(jnp.int32), (LAYERS, ZONAL))
        for r in range(BAND):
            for f in range(3):
                block, at = (own_first, f * 256 + r) if f < 2 else (own_rest, r)
                image = block[pl.ds(at, LAYERS, stride=BAND), :]
                image = jnp.take_along_axis(image, index, axis=1).reshape(2, 8, ZONAL)
                fields[f][r] = -image if f == 1 else image
            image = jnp.broadcast_to(own_rest[MASK - CUT + r : MASK - CUT + r + 1, :], (8, ZONAL))
            ms[r] = jnp.take_along_axis(image, index[:8], axis=1)

    coriolis_table(fs, position, core, sign)
    steps = fine_tools(fields, ps, ms, fs, coupling, depths)
    steps([(2 * t, (2 * t + 18, 2 * t + 17, 2 * t + 18)) for t in range(FINE_STEPS)])

    def row_of(r):
        return HALO + r + core * (BAND - 1 - 2 * r)

    root = jnp.sqrt(depths[...])
    jumps = []
    for f in range(3):
        rows = []
        for cr in range(4):
            here = [fields[f][row_of(4 * cr + r)].reshape(LAYERS, ZONAL) for r in range(4)]
            if f == 2:
                here = [sign * row for row in here]
            for r in range(4):
                fine[f * BAND + 4 * cr + r] = here[r]
            rows.append(here[0] + here[1] + here[2] + here[3])
        jumps.append(block_mean(rows) - following[f * LAYERS : (f + 1) * LAYERS, :])
    of_thickness = dot3(vectors[:, :LAYERS] / root, jumps[0])
    of_velocity = dot3(vectors[:, :LAYERS] * root, jnp.concatenate(jumps[1:], axis=1))
    for f, in_modes in enumerate((of_thickness, of_velocity[:, :ZONAL], of_velocity[:, ZONAL:])):
        chunk[pl.ds(f, LAYERS, stride=8), :] = in_modes
        chunk[pl.ds(4 + f, LAYERS, stride=8), :] = in_modes
    rows = []
    for cr in range(4):
        here = [ms[row_of(4 * cr + r)] for r in range(4)]
        rows.append(here[0] + here[1] + here[2] + here[3])
    chunk[pl.ds(3, BANDS, stride=4), :] = jnp.broadcast_to(block_mean(rows)[:1], (BANDS, ZONAL))


def coarse_tools(value, masks, fold):
    sub = iota((8, ZONAL), 0)
    lane = iota((8, ZONAL), 1)
    seg = lane % 4
    coriolis = []
    for cr in range(4):
        position = ((seg * 8 + sub) * 4 + cr).astype(F32)
        coriolis.append((4.0 * 0.3) * ((position + 0.5) / float(EXTENT // 4) - 0.5))
    keep = 1.0 - 4.0 * FRICTION
    k = fold[0, 0] // 4
    fold_index = 4 * ((k - lane // 4 + 32) % 32) + 3
    last, top = sub == 7, jnp.logical_and(sub == 7, seg == 3)
    first, bottom = sub == 0, jnp.logical_and(sub == 0, seg == 0)

    def east(x):
        return pltpu.roll(x, ZONAL - 4, 1) - pltpu.roll(x, 4, 1)

    def north(x, sign):
        up = pltpu.roll(x[0], 7, 0)
        up = jnp.where(last, pltpu.roll(up, ZONAL - 1, 1), up)
        up = jnp.where(top, sign * jnp.take_along_axis(x[3], fold_index, axis=1), up)
        down = pltpu.roll(x[3], 1, 0)
        down = jnp.where(first, pltpu.roll(down, 1, 1), down)
        down = jnp.where(bottom, 0.0, down)
        return [x[1] - down, x[2] - x[0], x[3] - x[1], up - x[2]]

    kept = [keep * m for m in masks]
    turned = [m * f for m, f in zip(masks, coriolis)]
    pushed = [(0.5 * value) * m for m in masks]
    spread = [0.5 * m for m in masks]

    def propagate(state):
        h, u, v = state
        for _ in range(2):
            north_h = north(h, 1.0)
            slow = [kept[i] * v[i] - pushed[i] * north_h[i] for i in range(4)]
            u = [(kept[i] * u[i] + turned[i] * v[i]) - pushed[i] * east(h[i]) for i in range(4)]
            v = [slow[i] - turned[i] * u[i] for i in range(4)]
            rest = [masks[i] * h[i] - spread[i] * east(u[i]) for i in range(4)]
            north_v = north(v, -1.0)
            h = [rest[i] - spread[i] * north_v[i] for i in range(4)]
        return [h, u, v]

    return propagate


def load_state(ref, begin=0):
    return [[ref[begin + f * 32 + cr * 8 : begin + f * 32 + cr * 8 + 8, :] for cr in range(4)] for f in range(3)]


def store_state(ref, state, begin=0):
    for f in range(3):
        for cr in range(4):
            ref[begin + f * 32 + cr * 8 : begin + f * 32 + cr * 8 + 8, :] = state[f][cr]


def add_state(a, b):
    return [[x + y for x, y in zip(p, q)] for p, q in zip(a, b)]


def load_masks(ref):
    return [ref[cr * 8 : cr * 8 + 8, :] for cr in range(4)]


PARTS = 7


def collect_kernel(spread, out):
    for part in range(PARTS):
        at = part + (28 if part > 3 else 0)
        both = [spread[pl.ds(core * 64 + at, 8, stride=4), :] for core in range(2)]
        out[part * 8 : part * 8 + 8, :] = jnp.where(core_index() == 0, both[0], both[1])


def pair_kernel(half, other_half, values, fold, jumps, mask_out, total):
    seg = iota((8, ZONAL), 1) % 4
    zh = lax.axis_index("zh")
    quarters = [(half, 0, zh), (half, PARTS * 8, zh ^ 3), (other_half, 0, zh ^ 1), (other_half, PARTS * 8, zh ^ 2)]
    for part in range(PARTS):
        rows = [None] * 4
        for ref, begin, quarter in quarters:
            piece = ref[begin + part * 8 : begin + part * 8 + 8, :]
            for cr in range(4):
                moved = pltpu.roll(piece, lax.rem(quarter - cr + ZONAL, ZONAL), 1)
                rows[cr] = moved if rows[cr] is None else jnp.where(seg == quarter, moved, rows[cr])
        for cr in range(4):
            if part == 3:
                mask_out[cr * 8 : cr * 8 + 8, :] = rows[cr]
            else:
                begin = (part if part < 3 else part - 1) * 32 + cr * 8
                jumps[begin : begin + 8, :] = rows[cr]
    propagate = coarse_tools(values[pl.ds(mode_index(), 1), :], load_masks(mask_out), fold)
    store_state(total, add_state(propagate(load_state(jumps)), load_state(jumps, 96)))


def group_kernel(total, mate, mask, values, fold, both):
    propagate = coarse_tools(values[pl.ds(mode_index(), 1), :], load_masks(mask), fold)
    odd = core_index() == 1
    mine, theirs = load_state(total), load_state(mate)
    earlier = [[jnp.where(odd, t, m) for m, t in zip(a, b)] for a, b in zip(mine, theirs)]
    later = [[jnp.where(odd, m, t) for m, t in zip(a, b)] for a, b in zip(mine, theirs)]
    trips = jnp.where(lax.axis_index("zl") < 3, 1, 0)
    state = lax.fori_loop(0, trips, lambda _, s: propagate(propagate(s)), earlier)
    store_state(both, add_state(state, later))


def repeat(wanted, propagate, state):
    return lax.fori_loop(0, jnp.where(wanted, 2, 0), lambda _, s: propagate(propagate(s)), state)


def earlier_kernel(three, mask, values, fold, out):
    propagate = coarse_tools(values[pl.ds(mode_index(), 1), :], load_masks(mask), fold)
    store_state(out, repeat(lax.axis_index("zl") == 3, propagate, load_state(three)))


def chain_kernel(one, two, earlier, mate, jumps, mask, values, fold, chunk):
    quarter = lax.axis_index("zh")
    core = core_index()
    propagate = coarse_tools(values[pl.ds(mode_index(), 1), :], load_masks(mask), fold)

    def twice(state):
        return propagate(propagate(state))

    state = add_state(load_state(earlier), load_state(two))
    state = repeat(lax.axis_index("zl") >= 2, propagate, state)
    state = add_state(state, load_state(one))
    state = lax.fori_loop(0, core, lambda _, s: add_state(twice(s), load_state(mate)), state)
    seg = iota((8, ZONAL), 1) % 4
    chunk[...] = jnp.zeros_like(chunk)
    for x in range(2):
        state = propagate(state)
        packed = []
        for f in range(3):
            pieces = [pltpu.roll(state[f][cr], lax.rem(cr - quarter + ZONAL, ZONAL), 1) for cr in range(4)]
            packed.append(pieces[0])
            for cr in range(1, 4):
                packed[f] = jnp.where(seg == cr, pieces[cr], packed[f])
        for which in range(2):
            for f in range(3):
                chunk[pl.ds((2 * which + x) * 32 + f, 8, stride=4), :] = jnp.where(core == which, packed[f], 0.0)
        if x == 0:
            state = add_state(state, load_state(jumps))


def correct_kernel(fine, gathered, vectors, depths, out, result, sems):
    half = lax.axis_index("x") // 2
    lanes = jnp.broadcast_to(depths[...], (LAYERS, LAYERS))
    eye = iota((LAYERS, LAYERS), 0) == iota((LAYERS, LAYERS), 1)
    root = jnp.sqrt(jnp.sum(jnp.where(eye, lanes, 0.0), axis=1, keepdims=True))
    lane = iota((LAYERS, ZONAL), 1)
    copies = []
    for f in range(3):
        in_modes = jnp.where(
            half == 0, gathered[pl.ds(f, LAYERS, stride=8), :], gathered[pl.ds(4 + f, LAYERS, stride=8), :]
        )
        (top, rest), (mode_top, mode_rest) = two_parts(in_modes), two_parts(vectors[:, :LAYERS])
        change = lax.dot_general(
            jnp.concatenate([mode_top, mode_top, mode_rest], axis=0),
            jnp.concatenate([top, rest, top], axis=0),
            (((0,), (0,)), ((), ())), preferred_element_type=F32,
        )
        change = change * root if f == 0 else change / root
        for cr in range(4):
            spread = jnp.take_along_axis(change, lane // 4 * 4 + cr, axis=1)
            for r in range(4):
                row = 4 * cr + r
                result[pl.ds(f * 256 + row, LAYERS, stride=BAND), :] = fine[f * BAND + row] + spread
        here = pl.ds(f * 256, 256)
        copies.append(pltpu.make_async_copy(result.at[here], out.at[here], sems.at[f]))
        copies[-1].start()
    for copy in copies:
        copy.wait()


def call(kernel, out_shapes, scratch=(), spaces=None, out_space=pltpu.VMEM, flops=1 << 20, vmem=24 << 20):
    def run(*arrays):
        specs = [pl.BlockSpec(memory_space=s) for s in spaces or (pltpu.VMEM,) * len(arrays)]
        return pl.pallas_call(
            kernel,
            out_shape=[jax.ShapeDtypeStruct(s, F32) for s in out_shapes],
            in_specs=specs,
            out_specs=[pl.BlockSpec(memory_space=out_space)] * len(out_shapes),
            scratch_shapes=list(scratch),
            compiler_params=pltpu.CompilerParams(vmem_limit_bytes=vmem),
            cost_estimate=pl.CostEstimate(flops=flops, bytes_accessed=1 << 20, transcendentals=0),
        )(*arrays)

    return run


def swap(block, axes):
    return lax.all_to_all(block, axes, 0, 0, tiled=True)


def body(start_state, land_mask, fold_map, coupling, depths):
    sent, first, rest, restricted = call(
        pack_kernel,
        [(MASK_AT + BAND, ZONAL), (CUT, ZONAL), (MASK + BAND - CUT, ZONAL), (3 * LAYERS, ZONAL)],
        [pltpu.SemaphoreType.DMA((3,))],
        spaces=(pl.ANY, pl.ANY),
    )(start_state.reshape(MASK, ZONAL), land_mask.astype(F32))
    fold = fold_map.reshape(1, ZONAL)
    depth_row = depths.reshape(1, LAYERS)
    across = [(i, i + 1) for i in range(1, BANDS - 1, 2)]
    across += [(b, a) for a, b in across]
    other = lax.ppermute(sent, SPACE, across)
    following = lax.ppermute(restricted, TIME, [(n + 1, n) for n in range(15)])
    vectors, values = call(modes_kernel, [(LAYERS, ZONAL), (LAYERS, ZONAL)], flops=10 << 20)(
        coupling, depth_row
    )
    inside = [(i, i ^ 1) for i in range(BANDS)]
    mate = [lax.ppermute(part, SPACE, inside) for part in (first, rest)]

    state = pltpu.VMEM((SPAN, 2, 8, ZONAL), F32)
    table = pltpu.VMEM((SPAN, 8, ZONAL), F32)
    scratch = [state, state, state, state, table, table]
    *inner, fold_held = call(
        inner_kernel, [(KEPT, 2, 8, ZONAL)] * 3 + [(1, ZONAL)], scratch, flops=4 << 20
    )(first, rest, *mate, fold, coupling, depth_row)
    fine, chunk = call(
        outer_kernel, [(3 * BAND, LAYERS, ZONAL), (4 * BANDS, ZONAL)], scratch
    )(
        first, rest, other, *inner, fold_held, coupling, depth_row, vectors, following
    )

    spread = swap(chunk, PLANE)
    (mine,) = call(collect_kernel, [(PARTS * 8, ZONAL)])(spread)
    beside = lax.ppermute(mine, ("zh",), [(i, i ^ 3) for i in range(4)])
    half = jnp.concatenate([mine, beside], axis=0)
    other_half = lax.ppermute(half, ("zh",), [(i, i ^ 1) for i in range(4)])
    jumps, mask, total = call(
        pair_kernel, [(192, ZONAL), (32, ZONAL), (96, ZONAL)]
    )(half, other_half, values, fold)
    mate = lax.ppermute(total, ("c",), [(0, 1), (1, 0)])
    (both,) = call(group_kernel, [(96, ZONAL)])(total, mate, mask, values, fold)
    three, two, one = (
        lax.ppermute(both, ("zl",), [(i, i + d) for i in range(4 - d)]) for d in (3, 2, 1)
    )
    (earlier,) = call(earlier_kernel, [(96, ZONAL)])(three, mask, values, fold)
    (chunk,) = call(chain_kernel, [(4 * BANDS, ZONAL)])(
        one, two, earlier, mate, jumps, mask, values, fold
    )
    change = swap(chunk, PLANE)
    (result,) = call(
        correct_kernel,
        [(MASK, ZONAL)],
        [pltpu.VMEM((MASK, ZONAL), F32), pltpu.SemaphoreType.DMA((3,))],
        out_space=pl.ANY,
    )(
        fine, change, vectors, depth_row
    )
    return result.reshape(1, 3, LAYERS, BAND, ZONAL)


def solution(mesh):
    parts = Mesh(mesh.devices.reshape(4, 4, 4, 4, 2), ("zl", "x", "zh", "y", "c"))
    return jax.shard_map(
        body,
        mesh=parts,
        in_specs=(P(TIME, None, None, SPACE, None), P(SPACE, None), P(), P(), P()),
        out_specs=P(TIME, None, None, SPACE, None),
        check_vma=False,
    )
```
